32 devices in a mesh: dp: 16 (over z, x, core), tensor: 2 (over y).
Axes of the slice: x: 2, y: 2, z: 4, core: 2. Of those that a mesh axis runs over, the one named last changes fastest.
Arguments:
- tokens: bfloat16 [16384, 2048], P(('dp', 'tensor')), may hold values from -6 to 6
- cotangent: bfloat16 [16384, 2048], P(('dp', 'tensor')), may hold values from -6 to 6
- routes: int32 [1, 16384, 2], P(None, 'dp'), may hold values from 0 to 3, all different within a row; in each aligned block of 1024 rows (0 to 1023, 1024 to 2047, ..., all dimensions but the last counted through in order) at most 576 rows name the same one
- route_weights: float32 [1, 16384, 2], P(None, 'dp'), may hold values from 0.3 to 1
- query_weight: bfloat16 [1, 2048, 4096], P(None, 'dp', 'tensor'), may hold values from -0.125 to 0.125
- key_weight: bfloat16 [1, 2048, 512], P(None, 'dp', 'tensor'), may hold values from -0.125 to 0.125
- value_weight: bfloat16 [1, 2048, 512], P(None, 'dp', 'tensor'), may hold values from -0.125 to 0.125
- out_weight: bfloat16 [1, 2048, 4096], P(None, 'dp', 'tensor'), may hold values from -0.375 to 0.375
- gate_weight: bfloat16 [1, 2048, 4, 768], P(None, 'dp', None, 'tensor'), may hold values from -0.125 to 0.125
- up_weight: bfloat16 [1, 2048, 4, 768], P(None, 'dp', None, 'tensor'), may hold values from -0.125 to 0.125
- down_weight: bfloat16 [1, 2048, 4, 768], P(None, 'dp', None, 'tensor'), may hold values from -0.625 to 0.625
- attn_gain: float32 [1, 2048], replicated, may hold values from 0.1 to 1.9
- ffn_gain: float32 [1, 2048], replicated, may hold values from 0.1 to 1.9
- query_gain: float32 [1, 128], replicated, may hold values from 0.1 to 1.9
- key_gain: float32 [1, 128], replicated, may hold values from 0.1 to 1.9
Outputs:
- layer_out: bfloat16 [16384, 2048], P(('dp', 'tensor'))
- tokens_grad: float32 [16384, 2048], P(('dp', 'tensor'))
- query_grad: float32 [1, 2048, 4096], P(None, 'dp', 'tensor')
- key_grad: float32 [1, 2048, 512], P(None, 'dp', 'tensor')
- value_grad: float32 [1, 2048, 512], P(None, 'dp', 'tensor')
- out_grad: float32 [1, 2048, 4096], P(None, 'dp', 'tensor')
- gate_grad: float32 [1, 2048, 4, 768], P(None, 'dp', None, 'tensor')
- up_grad: float32 [1, 2048, 4, 768], P(None, 'dp', None, 'tensor')
- down_grad: float32 [1, 2048, 4, 768], P(None, 'dp', None, 'tensor')
- attn_gain_grad: float32 [1, 2048], replicated
- ffn_gain_grad: float32 [1, 2048], replicated
- query_gain_grad: float32 [1, 128], replicated
- key_gain_grad: float32 [1, 128], replicated
The draws below stay inside these ranges and needn't reach their ends.
Inputs may be any that keep to these rules, and one draw needn't show every extreme that they name: `routes`: each row names 2 different experts; among the 1024 rows of one sequence in one layer no expert is named more than 576 times, and in some sequence some expert exactly 576 times.
All inputs are finite; a program needn't handle non-finite values.
Results may differ from the reference program's by a relative error of at most 0.02.
Values may be sent and summed in bfloat16 or wider, within the bound.
No kernel may reach another device: no remote copies, remote signals or barrier semaphores. Data moves between devices by JAX's collectives and lax.ppermute only.
A program may use at most 448 MiB of HBM per device.

```python
import math
import jax
import jax.numpy as jnp
import numpy as np
from jax import lax

D = 2048
H = 32
KV = 4
HD = 128
FF = 768
EXPERTS = 4
TOP = 2
LAYERS = 1
SEQ = 1024
TOKENS = 16384
CAP = 576
N_DP = 16


def block_levels(key, shape, shards, least, largest):
    level = 1.0
    for dim, blocks in shards:
        steps = jax.random.uniform(jax.random.fold_in(jax.random.fold_in(key, 6), dim), (blocks,), jnp.float32, least / len(shards), largest / len(shards))
        level = level * jnp.repeat(jnp.exp(steps), shape[dim] // blocks).reshape((-1,) + (1,) * (len(shape) - 1 - dim))
    return level


def assign_block(own_key, own, number, rows, number_of, top, bound, slope):
    ranking = jax.random.permutation(own_key, number_of)
    crowded, usual = portions_of(number_of, rows * top, bound, slope, True), portions_of(number_of, rows * top, bound, slope, False)
    places = jnp.arange(number_of)

    def named(sizes, rotation):
        used = int((sizes > 0).sum())
        fixed = max(1, used // 4)
        shifted = fixed + (places - fixed + rotation * (used - fixed)) % max(1, number_of - fixed)
        return jnp.zeros((number_of,), jnp.int32).at[ranking[jnp.where(places < fixed, places, shifted)]].set(jnp.asarray(sizes, jnp.int32))

    sizes = jnp.where(number % 4 == 0, named(crowded, number // 4), named(usual, number - number // 4 - 1))
    mixed = jax.random.permutation(jax.random.fold_in(own, 3), number_of)
    source_of, receiver = mixed[0:number_of // 2 * 2:2], mixed[1:number_of // 2 * 2:2]
    room = jnp.minimum(sizes[source_of] - 1, bound - sizes[receiver]) // 2
    room = jnp.where((source_of == ranking[0]) | (receiver == ranking[0]) | (sizes[receiver] == 0), 0, jnp.maximum(room, 0))
    shifted = jax.random.randint(jax.random.fold_in(own, 4), (number_of // 2,), 0, 1 << 20) % (room + 1)
    sizes = sizes.at[source_of].add(-shifted).at[receiver].add(shifted)
    members = jnp.searchsorted(jnp.cumsum(sizes), jnp.arange(rows * top), side="right").astype(jnp.int32)
    grid = members.reshape(top, rows).T
    grid = grid[jax.random.permutation(jax.random.fold_in(own, 1), rows)]
    rotation = jax.random.randint(jax.random.fold_in(own, 2), (rows, 1), 0, top)
    return jnp.take_along_axis(grid, (jnp.arange(top)[None, :] + rotation) % top, axis=1)


def portions_of(count, total, limit, slope, full):
    weights = [(1 << 20) // math.isqrt(grade ** slope) + 1 for grade in range(1, count + 1)]
    largest = limit if full else min(limit, max(-(-total // count), total * weights[0] // sum(weights)))
    least = 1 if total - largest >= count - 1 else 0
    holding, rest = [largest] + [least] * (count - 1), total - largest - least * (count - 1)
    while rest > 0:
        free = [i for i in range(1, count) if holding[i] < largest] or [i for i in range(1, count) if holding[i] < limit]
        whole, budget = sum([weights[i] for i in free]), rest
        for i in free:
            more = min(limit - holding[i], max(1, budget * weights[i] // whole), rest)
            holding[i] = holding[i] + more
            rest = rest - more
    return np.array(holding)


def normal_values(own_key, dims, width, bound, pieces=(), held_as=jnp.bfloat16):
    factor_of = block_levels(own_key, dims, pieces, -0.22, 0.18) if pieces else 1.0
    entries = jax.random.normal(own_key, dims, jnp.float32) * width * factor_of
    return jnp.minimum(jnp.maximum(entries, -bound), bound).astype(held_as)


def setup_inputs(seed: int = 0) -> dict:
    splits = jax.random.split(jax.random.key(seed), 16)
    tokens = normal_values(splits[0], (TOKENS, D), 1.0, 6.0, ((0, 32),))
    cotangent = normal_values(splits[1], (TOKENS, D), 1.0, 6.0, ((0, 32),))
    routes_keys = jax.random.split(jax.random.fold_in(splits[2], 1), LAYERS * TOKENS // SEQ)
    routes_turns = jax.random.permutation(jax.random.fold_in(splits[2], 3), LAYERS * TOKENS // SEQ)
    routes = jax.vmap(lambda own, number: assign_block(jax.random.fold_in(splits[2], 2), own, number, SEQ, EXPERTS, TOP, CAP, 1))(routes_keys, routes_turns).reshape((LAYERS, TOKENS, TOP))
    route_weights = jnp.clip(jnp.exp(math.log(1.0) - 1.2039728 * jax.random.uniform(splits[3], (LAYERS, TOKENS, TOP), jnp.float32) ** block_levels(splits[3], (LAYERS, TOKENS, TOP), ((1, 16),), -0.2, 0.2)), 0.3, 1.0)
    query_weight = normal_values(splits[4], (LAYERS, D, H * HD), D ** -0.5, 0.125, ((1, 16), (2, 2)))
    key_weight = normal_values(splits[5], (LAYERS, D, KV * HD), D ** -0.5, 0.125, ((1, 16), (2, 2)))
    value_weight = normal_values(splits[6], (LAYERS, D, KV * HD), D ** -0.5, 0.125, ((1, 16), (2, 2)))
    out_weight = normal_values(splits[7], (LAYERS, D, H * HD), (H * HD // 16) ** -0.5, 0.375, ((1, 16), (2, 2)))
    gate_weight = normal_values(splits[8], (LAYERS, D, EXPERTS, FF), D ** -0.5, 0.125, ((1, 16), (3, 2)))
    up_weight = normal_values(splits[9], (LAYERS, D, EXPERTS, FF), D ** -0.5, 0.125, ((1, 16), (3, 2)))
    down_weight = normal_values(splits[10], (LAYERS, D, EXPERTS, FF), (FF // 8) ** -0.5, 0.625, ((1, 16), (3, 2)))
    attn_gain = jnp.clip(1.0 + 0.18 * jax.random.normal(splits[11], (LAYERS, D), jnp.float32), 0.1, 1.9)
    ffn_gain = jnp.clip(1.0 + 0.18 * jax.random.normal(splits[12], (LAYERS, D), jnp.float32), 0.1, 1.9)
    query_gain = jnp.clip(1.0 + 0.18 * jax.random.normal(splits[13], (LAYERS, HD), jnp.float32), 0.1, 1.9)
    key_gain = jnp.clip(1.0 + 0.18 * jax.random.normal(splits[14], (LAYERS, HD), jnp.float32), 0.1, 1.9)
    return {"tokens": tokens, "cotangent": cotangent, "routes": routes, "route_weights": route_weights, "query_weight": query_weight, "key_weight": key_weight, "value_weight": value_weight, "out_weight": out_weight, "gate_weight": gate_weight, "up_weight": up_weight, "down_weight": down_weight, "attn_gain": attn_gain, "ffn_gain": ffn_gain, "query_gain": query_gain, "key_gain": key_gain}


EPS = 1e-06
THETA = 1000000.0
HIGH = lax.Precision.HIGHEST

@jax.custom_vjp
def low(v):
    return lax.optimization_barrier(v.astype(jnp.bfloat16)).astype(jnp.float32)

@jax.custom_vjp
def low_back(v):
    return v

def low_keep(v):
    return (low(v), None)

def low_pass(kept, grad):
    return (grad,)

def back_keep(v):
    return (v, None)

def back_low(kept, grad):
    return (low(grad),)
low.defvjp(low_keep, low_pass)
low_back.defvjp(back_keep, back_low)

def rms_norm(values, gain):
    return values * lax.rsqrt(lax.optimization_barrier(jnp.mean(values * values, axis=-1, keepdims=True)) + EPS) * gain

def rotate(values, cosine, sine):
    half = values.shape[-1] // 2
    first = values[..., :half]
    second = values[..., half:]
    return jnp.concatenate([first * cosine - second * sine, second * cosine + first * sine], axis=-1)

def decoder_layer(resid, params, route_rows, weight_rows):
    query_w, key_w, value_w, out_w, gate_w, up_w, down_w, attn_g, ffn_g, query_g, key_g = params
    batch = resid.shape[0]
    position = jnp.arange(SEQ).astype(jnp.float32)
    freq = THETA ** (-2.0 * jnp.arange(HD // 2).astype(jnp.float32) / HD)
    angle = position[:, None] * freq[None, :]
    cosine = jnp.cos(angle)[:, None, :]
    sine = jnp.sin(angle)[:, None, :]
    normed = low(rms_norm(resid, attn_g))
    query = low_back(jnp.matmul(normed, query_w, precision=HIGH)).reshape(batch, SEQ, H, HD)
    keys = low_back(jnp.matmul(normed, key_w, precision=HIGH)).reshape(batch, SEQ, KV, HD)
    values = low(low_back(jnp.matmul(normed, value_w, precision=HIGH))).reshape(batch, SEQ, KV, HD)
    query = low(rotate(rms_norm(query, query_g), cosine, sine)).reshape(batch, SEQ, KV, H // KV, HD)
    keys = low(rotate(rms_norm(keys, key_g), cosine, sine))
    scores = low_back(jnp.einsum('bqkgh,bpkh->bkgqp', query, keys, precision=HIGH) * HD ** (-0.5))
    causal = jnp.arange(SEQ)[:, None] >= jnp.arange(SEQ)[None, :]
    scores = jnp.where(causal, scores, -1e+30)
    probs = jnp.exp(scores - jax.scipy.special.logsumexp(scores, axis=-1, keepdims=True))
    context = jnp.einsum('bkgqp,bpkh->bqkgh', low(probs), values, precision=HIGH).reshape(batch, SEQ, H * HD)
    context = low(low_back(context))
    resid = resid + low_back(jnp.einsum('bsc,dc->bsd', context, out_w, precision=HIGH))
    normed = low(rms_norm(resid, ffn_g))
    share = lax.optimization_barrier(jnp.sum(weight_rows[..., None] * (route_rows[..., None] == jnp.arange(EXPERTS, dtype=jnp.int32)), axis=-2))
    gate_val = low_back(jnp.einsum('bsd,def->bsef', normed, gate_w, precision=HIGH))
    up_val = low_back(jnp.einsum('bsd,def->bsef', normed, up_w, precision=HIGH))
    hidden = low(jax.nn.silu(gate_val) * up_val * share[..., None])
    return resid + low_back(jnp.einsum('bsef,def->bsd', hidden, down_w, precision=HIGH))

def reference(tokens, cotangent, routes, route_weights, query_weight, key_weight, value_weight, out_weight, gate_weight, up_weight, down_weight, attn_gain, ffn_gain, query_gain, key_gain):
    params = tuple((weight.astype(jnp.float32) for weight in (query_weight, key_weight, value_weight, out_weight, gate_weight, up_weight, down_weight, attn_gain, ffn_gain, query_gain, key_gain)))
    batch = math.gcd(N_DP, max(1, 2048 // SEQ))
    blocks = N_DP // batch
    inputs = tokens.astype(jnp.float32).reshape(blocks, batch, SEQ, D)
    grads = cotangent.astype(jnp.float32).reshape(blocks, batch, SEQ, D)
    route_blocks = routes.reshape(LAYERS, blocks, batch, SEQ, TOP).transpose(1, 0, 2, 3, 4)
    weight_blocks = route_weights.astype(jnp.float32).reshape(LAYERS, blocks, batch, SEQ, TOP).transpose(1, 0, 2, 3, 4)

    def forward(weights, resid, route_part, weight_part):
        for layer in range(LAYERS):
            resid = decoder_layer(resid, tuple((weight[layer] for weight in weights)), route_part[layer], weight_part[layer])
        return resid

    def one_block(totals, items):
        resid, grad, route_part, weight_part = items
        output, pullback = jax.vjp(lambda weights, start: forward(weights, start, route_part, weight_part), params, resid)
        weight_grads, input_grad = pullback(grad)
        totals = jax.tree.map(lambda total, part: total + part, totals, weight_grads)
        return (totals, (output, input_grad))
    zeros = jax.tree.map(jnp.zeros_like, params)
    totals, (outputs, input_grads) = lax.scan(one_block, zeros, (inputs, grads, route_blocks, weight_blocks))
    return (outputs.reshape(TOKENS, D).astype(jnp.bfloat16), input_grads.reshape(TOKENS, D), totals[0], totals[1], totals[2], totals[3], totals[4], totals[5], totals[6], totals[7], totals[8], totals[9], totals[10])
```

```python
import functools
import math

import jax
import jax.numpy as jnp
import numpy as np
from jax import lax
from jax.experimental import pallas as pl
from jax.experimental.pallas import tpu as pltpu
from jax.sharding import PartitionSpec as P

HD = 128
EPS = 1e-06
SCALE = HD ** -0.5
LOG2E = math.log2(math.e)
NT = (((1,), (1,)), ((), ()))


def head_norm(values, gain, cosine, sine):
    scale = lax.rsqrt(jnp.mean(values * values, axis=-1, keepdims=True) + EPS)
    normed = values * scale * gain
    return normed * cosine + pltpu.roll(normed, HD // 2, 1) * sine, scale


def head_norm_back(values, scale, gain, cosine, sine, grad_rot):
    grad = grad_rot * cosine - pltpu.roll(grad_rot, HD // 2, 1) * sine
    scaled = grad * gain
    inner = jnp.mean(scaled * values, axis=-1, keepdims=True)
    grad_values = scale * scaled - values * (scale * scale * scale) * inner
    return grad_values, jnp.sum(grad * values * scale, axis=0, keepdims=True)


def causal_mask(block):
    key = lax.broadcasted_iota(jnp.int32, (block, block), 0)
    query = lax.broadcasted_iota(jnp.int32, (block, block), 1)
    return key <= query


def attn_fwd_kernel(block, q_ref, k_ref, v_ref, qg_ref, kg_ref, cos_ref, sin_ref, out_ref, lse_ref, qs, ks, vt, ps):
    seq = q_ref.shape[0]

    @pl.when(pl.program_id(1) == 0)
    def _():
        ks[...] = head_norm(k_ref[...], kg_ref[...], cos_ref[...], sin_ref[...])[0].astype(jnp.bfloat16)
        vt[...] = v_ref[...].astype(jnp.bfloat16).T

    qs[...] = head_norm(q_ref[...], qg_ref[...], cos_ref[...], sin_ref[...])[0].astype(jnp.bfloat16)
    mask = causal_mask(block)
    for i in range(seq // block):
        cols = slice(i * block, (i + 1) * block)
        total = jnp.zeros((1, block), jnp.float32)
        for j in range(i + 1):
            rows = slice(j * block, (j + 1) * block)
            scores = lax.dot_general(ks[rows], qs[cols], NT, preferred_element_type=jnp.float32)
            probs = jnp.exp2(scores * (SCALE * LOG2E))
            if j == i:
                probs = jnp.where(mask, probs, 0.0)
            total = total + jnp.sum(probs, axis=0, keepdims=True)
            ps[rows, cols] = probs.astype(jnp.bfloat16)
        lse_ref[0, :, cols] = jnp.log2(total)
        end = (i + 1) * block
        mixed = jnp.dot(vt[:, :end], ps[:end, cols], preferred_element_type=jnp.float32)
        out_ref[cols, :] = (mixed * (1.0 / total)).T.astype(jnp.bfloat16)


def attention_fwd(raw, q_cols, kv_cols, query_g, key_g, cosine, sine):
    seq = raw.shape[0]
    heads, kv = q_cols // HD, kv_cols // HD
    group = heads // kv
    block = min(256, seq)
    head = pl.BlockSpec((seq, HD), lambda k, g: (0, k * group + g))
    key = pl.BlockSpec((seq, HD), lambda k, g: (0, k))
    key_in = pl.BlockSpec((seq, HD), lambda k, g: (0, heads + k))
    value_in = pl.BlockSpec((seq, HD), lambda k, g: (0, heads + kv + k))
    gain = pl.BlockSpec((1, HD), lambda k, g: (0, 0))
    table = pl.BlockSpec((seq, HD), lambda k, g: (0, 0))
    return pl.pallas_call(
        functools.partial(attn_fwd_kernel, block),
        grid=(kv, group),
        in_specs=[head, key_in, value_in, gain, gain, table, table],
        out_specs=[head, pl.BlockSpec((1, 1, seq), lambda k, g: (k * group + g, 0, 0))],
        out_shape=[
            jax.ShapeDtypeStruct((seq, heads * HD), jnp.bfloat16),
            jax.ShapeDtypeStruct((heads, 1, seq), jnp.float32),
        ],
        scratch_shapes=[
            pltpu.VMEM((seq, HD), jnp.bfloat16),
            pltpu.VMEM((seq, HD), jnp.bfloat16),
            pltpu.VMEM((HD, seq), jnp.bfloat16),
            pltpu.VMEM((seq, seq), jnp.bfloat16),
        ],
        compiler_params=pltpu.CompilerParams(vmem_limit_bytes=40 * 2**20),
    )(raw, raw, raw, query_g, key_g, cosine, sine)


def attn_bwd_kernel(
    block, q_ref, k_ref, v_ref, ctx_ref, grad_ref, lse_ref, qg_ref, kg_ref, cos_ref, sin_ref,
    dq_ref, dk_ref, dv_ref, dqg_ref, dkg_ref,
    qs, ks, kt, vs, ps, ds, dks, dvs,
):
    seq = q_ref.shape[0]
    kv_id, g_id = pl.program_id(0), pl.program_id(1)

    @pl.when(g_id == 0)
    def _():
        rotated = head_norm(k_ref[...], kg_ref[...], cos_ref[...], sin_ref[...])[0].astype(jnp.bfloat16)
        ks[...] = rotated
        kt[...] = rotated.T
        vs[...] = v_ref[...].astype(jnp.bfloat16)
        dks[...] = jnp.zeros_like(dks)
        dvs[...] = jnp.zeros_like(dvs)

    @pl.when((g_id == 0) & (kv_id == 0))
    def _():
        dqg_ref[...] = jnp.zeros_like(dqg_ref)
        dkg_ref[...] = jnp.zeros_like(dkg_ref)

    qs[...] = head_norm(q_ref[...], qg_ref[...], cos_ref[...], sin_ref[...])[0].astype(jnp.bfloat16)
    mask = causal_mask(block)
    count = seq // block
    for i in range(count):
        cols = slice(i * block, (i + 1) * block)
        product = grad_ref[cols].astype(jnp.float32) * ctx_ref[cols].astype(jnp.float32)
        delta = jnp.sum(product.T, axis=0, keepdims=True)
        lse = lse_ref[0, :, cols]
        for j in range(i + 1):
            rows = slice(j * block, (j + 1) * block)
            scores = lax.dot_general(ks[rows], qs[cols], NT, preferred_element_type=jnp.float32)
            probs = jnp.exp2(scores * (SCALE * LOG2E) - lse)
            if j == i:
                probs = jnp.where(mask, probs, 0.0)
            grad_probs = lax.dot_general(vs[rows], grad_ref[cols], NT, preferred_element_type=jnp.float32)
            ps[rows, cols] = probs.astype(jnp.bfloat16)
            ds[rows, cols] = (probs * (grad_probs - delta)).astype(jnp.bfloat16)
    for j in range(count):
        rows = slice(j * block, (j + 1) * block)
        dvs[rows] += jnp.dot(ps[rows, j * block :], grad_ref[j * block :], preferred_element_type=jnp.float32)
        dks[rows] += jnp.dot(ds[rows, j * block :], qs[j * block :], preferred_element_type=jnp.float32)
    gain_sum = jnp.zeros((1, HD), jnp.float32)
    for i in range(count):
        cols = slice(i * block, (i + 1) * block)
        end = (i + 1) * block
        grad_t = jnp.dot(kt[:, :end], ds[:end, cols], preferred_element_type=jnp.float32)
        raw = q_ref[cols]
        scale = lax.rsqrt(jnp.mean(raw * raw, axis=-1, keepdims=True) + EPS)
        grad_raw, part = head_norm_back(raw, scale, qg_ref[...], cos_ref[cols], sin_ref[cols], grad_t.T * SCALE)
        dq_ref[cols] = grad_raw.astype(jnp.bfloat16)
        gain_sum = gain_sum + part
    dqg_ref[...] += gain_sum

    @pl.when(g_id == pl.num_programs(1) - 1)
    def _():
        raw = k_ref[...]
        scale = lax.rsqrt(jnp.mean(raw * raw, axis=-1, keepdims=True) + EPS)
        grad_raw, part = head_norm_back(raw, scale, kg_ref[...], cos_ref[...], sin_ref[...], dks[...] * SCALE)
        dk_ref[...] = grad_raw.astype(jnp.bfloat16)
        dv_ref[...] = dvs[...].astype(jnp.bfloat16)
        dkg_ref[...] += part


def attention_bwd(raw, q_cols, kv_cols, context, grad_context, lse, query_g, key_g, cosine, sine):
    seq = raw.shape[0]
    heads, kv = q_cols // HD, kv_cols // HD
    group = heads // kv
    block = min(256, seq)
    head = pl.BlockSpec((seq, HD), lambda k, g: (0, k * group + g))
    key = pl.BlockSpec((seq, HD), lambda k, g: (0, k))
    key_in = pl.BlockSpec((seq, HD), lambda k, g: (0, heads + k))
    value_in = pl.BlockSpec((seq, HD), lambda k, g: (0, heads + kv + k))
    gain = pl.BlockSpec((1, HD), lambda k, g: (0, 0))
    table = pl.BlockSpec((seq, HD), lambda k, g: (0, 0))
    return pl.pallas_call(
        functools.partial(attn_bwd_kernel, block),
        grid=(kv, group),
        in_specs=[head, key_in, value_in, head, head, pl.BlockSpec((1, 1, seq), lambda k, g: (k * group + g, 0, 0)),
                  gain, gain, table, table],
        out_specs=[head, key, key, gain, gain],
        out_shape=[
            jax.ShapeDtypeStruct((seq, heads * HD), jnp.bfloat16),
            jax.ShapeDtypeStruct((seq, kv * HD), jnp.bfloat16),
            jax.ShapeDtypeStruct((seq, kv * HD), jnp.bfloat16),
            jax.ShapeDtypeStruct((1, HD), jnp.float32),
            jax.ShapeDtypeStruct((1, HD), jnp.float32),
        ],
        scratch_shapes=[
            pltpu.VMEM((seq, HD), jnp.bfloat16),
            pltpu.VMEM((seq, HD), jnp.bfloat16),
            pltpu.VMEM((HD, seq), jnp.bfloat16),
            pltpu.VMEM((seq, HD), jnp.bfloat16),
            pltpu.VMEM((seq, seq), jnp.bfloat16),
            pltpu.VMEM((seq, seq), jnp.bfloat16),
            pltpu.VMEM((seq, HD), jnp.float32),
            pltpu.VMEM((seq, HD), jnp.float32),
        ],
        compiler_params=pltpu.CompilerParams(vmem_limit_bytes=48 * 2**20),
    )(raw, raw, raw, context, grad_context, lse, query_g, key_g, cosine, sine)


def rope_tables(seq):
    position = lax.iota(jnp.float32, seq)
    freq = 1000000.0 ** (-2.0 * lax.iota(jnp.float32, HD // 2) / HD)
    angle = position[:, None] * freq[None, :]
    cosine, sine = jnp.cos(angle), jnp.sin(angle)
    return jnp.concatenate([cosine, cosine], axis=1), jnp.concatenate([-sine, sine], axis=1)

BF = jnp.bfloat16
F32 = jnp.float32


def dot(left, right):
    return jnp.dot(left, right, preferred_element_type=F32)


def dot_nt(left, right):
    return lax.dot_general(left, right, (((1,), (1,)), ((), ())), preferred_element_type=F32)


def dot_tn(left, right):
    return lax.dot_general(left, right, (((0,), (0,)), ((), ())), preferred_element_type=F32)


def bits_of(count):
    return count.bit_length() - 1


def swap(value, bit):
    count = lax.axis_size("dp")
    return lax.ppermute(value, "dp", [(i, i ^ (1 << bit)) for i in range(count)])


def swap_pair(value):
    return lax.ppermute(value, "tensor", [(0, 1), (1, 0)])


def block_order():
    count = lax.axis_size("dp")
    bits = bits_of(count)
    reverse = np.array([int(format(i, "b").zfill(bits)[::-1], 2) if bits else 0 for i in range(count)], np.int32)
    me = lax.axis_index("dp").astype(jnp.int32)
    return jnp.asarray(reverse) ^ me, jnp.asarray(reverse)[lax.iota(jnp.int32, count) ^ me]


def copy_kernel(order_ref, in_ref, out_ref):
    out_ref[...] = in_ref[...]


def reorder(values, order):
    rows, width = values.shape
    count = order.shape[0]
    block = width // count
    if block % 128 or rows % 16:
        return jnp.take(values.reshape(rows, count, block), order, axis=1).reshape(rows, width)
    return pl.pallas_call(
        copy_kernel,
        grid_spec=pltpu.PrefetchScalarGridSpec(
            num_scalar_prefetch=1,
            grid=(count,),
            in_specs=[pl.BlockSpec((rows, block), lambda i, order_ref: (0, order_ref[i]))],
            out_specs=pl.BlockSpec((rows, block), lambda i, order_ref: (0, i)),
        ),
        out_shape=jax.ShapeDtypeStruct(values.shape, values.dtype),
    )(order, values)


def gather_rows(shard):
    block = shard
    for bit in reversed(range(bits_of(lax.axis_size("dp")))):
        block = jnp.concatenate([block, swap(block, bit)], axis=0)
    return block


def reduce_rows(left, right):
    bits = bits_of(lax.axis_size("dp"))
    half = left.shape[1] // 2
    received = swap(dot_tn(left[:, half:], right).astype(BF), 0)
    keep = dot_tn(left[:, :half], right) + received.astype(F32)
    for bit in range(1, bits):
        half = keep.shape[0] // 2
        received = swap(keep[half:].astype(BF), bit)
        keep = keep[:half] + received.astype(F32)
        if bit < bits - 1:
            keep = keep.astype(BF).astype(F32)
    return keep


def sum_all(value):
    for bit in range(bits_of(lax.axis_size("dp"))):
        value = value + swap(value, bit)
    return value + swap_pair(value)


def both_rows(own, turn):
    other = swap_pair(own)
    return jnp.where(turn == 0, jnp.concatenate([own, other], axis=0), jnp.concatenate([other, own], axis=0))


def rms_scale(values):
    return lax.rsqrt(jnp.mean(values * values, axis=-1, keepdims=True) + EPS)


def norm_back(values, scale, gain, grad):
    scaled = grad * gain
    inner = jnp.mean(scaled * values, axis=-1, keepdims=True)
    grad_values = scale * scaled - values * (scale * scale * scale) * inner
    return (grad_values, jnp.sum(grad * values * scale, axis=0, keepdims=True))


def body(
    tokens, cotangent, routes, route_weights, query_weight, key_weight, value_weight, out_weight,
    gate_weight, up_weight, down_weight, attn_gain, ffn_gain, query_gain, key_gain,
):
    turn = lax.axis_index("tensor")
    own = tokens.shape[0]
    seq = 2 * own
    width = tokens.shape[1]
    order, inverse = block_order()
    cosine, sine = rope_tables(seq)
    experts, hidden_cols = gate_weight.shape[2], gate_weight.shape[3]
    flat = experts * hidden_cols
    q_cols, kv_cols = query_weight.shape[2], key_weight.shape[2]

    def mine(values):
        return lax.dynamic_slice_in_dim(values, turn * own, own, axis=0)

    def theirs(values):
        return lax.dynamic_slice_in_dim(values, (1 - turn) * own, own, axis=0)

    qkv_w = gather_rows(jnp.concatenate([query_weight[0], key_weight[0], value_weight[0]], axis=1))
    out_w = gather_rows(out_weight[0])
    down_w = gather_rows(down_weight[0].reshape(-1, flat))
    gate_up_w = gather_rows(
        jnp.concatenate([gate_weight[0].reshape(-1, flat), up_weight[0].reshape(-1, flat)], axis=1)
    )

    tokens_all = reorder(both_rows(tokens, turn), order)
    grad_b = reorder(both_rows(cotangent, turn), order)
    attn_g = reorder(attn_gain, order)
    ffn_g = reorder(ffn_gain, order)

    resid = tokens_all.astype(F32)
    scale_one = rms_scale(resid)
    normed = (resid * scale_one * attn_g).astype(BF)
    raw = dot(normed, qkv_w)
    context, lse = attention_fwd(raw, q_cols, kv_cols, query_gain, key_gain, cosine, sine)

    share = jnp.sum(
        route_weights[0][:, :, None] * (routes[0][:, :, None] == lax.iota(jnp.int32, experts)).astype(F32), axis=1
    )
    share = jnp.broadcast_to(share[:, :, None], (seq, experts, hidden_cols)).reshape(seq, flat)
    grad_hidden = dot(grad_b, down_w)

    chunk = seq // 2
    mids = []
    for start in range(0, seq, chunk):
        part = dot_nt(context[start : start + chunk], out_w)
        mids.append(resid[start : start + chunk] + part + swap_pair(part.astype(BF)).astype(F32))
    mid = jnp.concatenate(mids, axis=0)
    scale_two = rms_scale(mid)
    normed_f = (mid * scale_two * ffn_g).astype(BF)
    gate_up = dot(normed_f, gate_up_w)
    gate, up = gate_up[:, :flat], gate_up[:, flat:]
    sigma = jax.nn.sigmoid(gate)
    hidden = (gate * sigma * up * share).astype(BF)
    shared = grad_hidden * share
    grad_gate = (shared * up * sigma * (1.0 + gate * (1.0 - sigma))).astype(BF)
    grad_up = (shared * (gate * sigma)).astype(BF)
    grad_gate_up = jnp.concatenate([grad_gate, grad_up], axis=1)

    grads_mid = []
    ffn_part = jnp.zeros((1, width), F32)
    for start in range(0, seq, chunk):
        rows = slice(start, start + chunk)
        part = dot_nt(grad_gate_up[rows], gate_up_w)
        total = part + swap_pair(part.astype(BF)).astype(F32)
        back, gain_part = norm_back(mid[rows], scale_two[rows], ffn_g, total)
        ffn_part = ffn_part + gain_part
        grads_mid.append(grad_b[rows].astype(F32) + back)
    grad_mid = jnp.concatenate(grads_mid, axis=0)
    grad_mid_b = grad_mid.astype(BF)

    gate_up_grad = reduce_rows(normed_f, grad_gate_up)
    down_grad = reduce_rows(grad_b, hidden)
    out_theirs = swap_pair(dot_nt(theirs(hidden), down_w).astype(BF)).astype(F32)
    output = (mine(mid) + dot_nt(mine(hidden), down_w) + out_theirs).astype(BF)

    out_grad = reduce_rows(grad_mid_b, context)
    grad_context = dot(grad_mid_b, out_w).astype(BF)
    dq, dk, dv, query_part, key_part = attention_bwd(
        raw, q_cols, kv_cols, context, grad_context, lse, query_gain, key_gain, cosine, sine
    )
    grad_qkv = jnp.concatenate([dq, dk, dv], axis=1)
    qkv_grad = reduce_rows(normed, grad_qkv)
    normed_theirs = swap_pair(dot_nt(theirs(grad_qkv), qkv_w).astype(BF)).astype(F32)
    grad_normed = dot_nt(mine(grad_qkv), qkv_w) + normed_theirs
    grad_one, attn_part = norm_back(mine(resid), mine(scale_one), attn_g, grad_normed)
    tokens_grad = reorder(mine(grad_mid) + grad_one, inverse)

    small = jnp.concatenate(
        [reorder(attn_part, inverse), reorder(ffn_part * 0.5, inverse), query_part, key_part], axis=1
    )
    small = sum_all(small)
    attn_total, ffn_total = small[:, :width], small[:, width : 2 * width]
    query_total, key_total = small[:, 2 * width : 2 * width + HD], small[:, 2 * width + HD :]

    def expert(values):
        return values.reshape(1, -1, experts, hidden_cols)

    return (
        reorder(output, inverse),
        tokens_grad,
        qkv_grad[None, :, :q_cols],
        qkv_grad[None, :, q_cols : q_cols + kv_cols],
        qkv_grad[None, :, q_cols + kv_cols :],
        out_grad[None],
        expert(gate_up_grad[:, :flat]),
        expert(gate_up_grad[:, flat:]),
        expert(down_grad),
        attn_total,
        ffn_total,
        query_total,
        key_total,
    )


def solution(mesh):
    return jax.shard_map(
        body,
        mesh=mesh,
        in_specs=(
            P(("dp", "tensor"), None),
            P(("dp", "tensor"), None),
            P(None, "dp", None),
            P(None, "dp", None),
            P(None, "dp", "tensor"),
            P(None, "dp", "tensor"),
            P(None, "dp", "tensor"),
            P(None, "dp", "tensor"),
            P(None, "dp", None, "tensor"),
            P(None, "dp", None, "tensor"),
            P(None, "dp", None, "tensor"),
            P(),
            P(),
            P(),
            P(),
        ),
        out_specs=(
            P(("dp", "tensor"), None),
            P(("dp", "tensor"), None),
            P(None, "dp", "tensor"),
            P(None, "dp", "tensor"),
            P(None, "dp", "tensor"),
            P(None, "dp", "tensor"),
            P(None, "dp", None, "tensor"),
            P(None, "dp", None, "tensor"),
            P(None, "dp", None, "tensor"),
            P(),
            P(),
            P(),
            P(),
        ),
        check_vma=False,
    )
```

```python
import functools
import math

import jax
import jax.numpy as jnp
import numpy as np
from jax import lax
from jax.experimental import pallas as pl
from jax.experimental.pallas import tpu as pltpu
from jax.sharding import PartitionSpec as P

HD = 128
EPS = 1e-06
THETA = 1000000.0
SCALE = HD ** -0.5
LOG2E = math.log2(math.e)
NT = (((1,), (1,)), ((), ()))
BF = jnp.bfloat16
F32 = jnp.float32


def params(mib):
    return pltpu.CompilerParams(vmem_limit_bytes=mib * 2**20)


def dot(left, right):
    return jnp.dot(left, right, preferred_element_type=F32)


def dot_nt(left, right):
    return lax.dot_general(left, right, NT, preferred_element_type=F32)


def dot_tn(left, right):
    return lax.dot_general(left, right, (((0,), (0,)), ((), ())), preferred_element_type=F32)


def head_norm(values, gain, cosine, sine):
    scale = lax.rsqrt(jnp.mean(values * values, axis=-1, keepdims=True) + EPS)
    normed = values * scale * gain
    return normed * cosine + pltpu.roll(normed, HD // 2, 1) * sine


def head_norm_back(values, gain, cosine, sine, grad_rot):
    scale = lax.rsqrt(jnp.mean(values * values, axis=-1, keepdims=True) + EPS)
    grad = grad_rot * cosine - pltpu.roll(grad_rot, HD // 2, 1) * sine
    scaled = grad * gain
    inner = jnp.mean(scaled * values, axis=-1, keepdims=True)
    grad_values = scale * scaled - values * (scale * scale * scale) * inner
    return grad_values, jnp.sum(grad * values * scale, axis=0, keepdims=True)


def causal_mask(block):
    key = lax.broadcasted_iota(jnp.int32, (block, block), 0)
    query = lax.broadcasted_iota(jnp.int32, (block, block), 1)
    return key <= query


def attn_fwd_kernel(
    block, q_ref, k_ref, v_ref, qg_ref, kg_ref, qcos_ref, qsin_ref, kcos_ref, ksin_ref, out_ref, lse_ref, qs, ks, vt, ps
):
    base = (k_ref.shape[0] - q_ref.shape[0]) // block

    @pl.when(pl.program_id(1) == 0)
    def _():
        ks[...] = head_norm(k_ref[...], kg_ref[...], kcos_ref[...], ksin_ref[...]).astype(BF)
        vt[...] = v_ref[...].astype(BF).T

    qs[...] = head_norm(q_ref[...], qg_ref[...], qcos_ref[...], qsin_ref[...]).astype(BF)
    mask = causal_mask(block)
    for i in range(q_ref.shape[0] // block):
        cols = slice(i * block, (i + 1) * block)
        total = jnp.zeros((1, block), F32)
        for j in range(base + i + 1):
            rows = slice(j * block, (j + 1) * block)
            probs = jnp.exp2(dot_nt(ks[rows], qs[cols]) * (SCALE * LOG2E))
            if j == base + i:
                probs = jnp.where(mask, probs, 0.0)
            total = total + jnp.sum(probs, axis=0, keepdims=True)
            ps[rows, cols] = probs.astype(BF)
        lse_ref[0, :, cols] = jnp.log2(total)
        end = (base + i + 1) * block
        mixed = dot(vt[:, :end], ps[:end, cols])
        out_ref[cols, :] = (mixed * (1.0 / total)).T.astype(BF)


def attn_specs(raw, q_cols, kv_cols, chunk, index):
    heads, kv = q_cols // HD, kv_cols // HD
    group = heads // kv
    keys = (index + 1) * chunk
    head_in = pl.BlockSpec((chunk, HD), lambda k, g: (index, k * group + g))
    head = pl.BlockSpec((chunk, HD), lambda k, g: (0, k * group + g))
    lse = pl.BlockSpec((1, 1, chunk), lambda k, g: (k * group + g, 0, 0))
    gain = pl.BlockSpec((1, HD), lambda k, g: (0, 0))
    query_table = pl.BlockSpec((chunk, HD), lambda k, g: (index, 0))

    def of_keys(rows):
        return (
            pl.BlockSpec((rows, HD), lambda k, g: (0, heads + k)),
            pl.BlockSpec((rows, HD), lambda k, g: (0, heads + kv + k)),
            pl.BlockSpec((rows, HD), lambda k, g: (0, 0)),
            pl.BlockSpec((rows, HD), lambda k, g: (0, k)),
        )

    return heads, kv, group, keys, head_in, head, lse, gain, query_table, of_keys


def attention_fwd(raw, q_cols, kv_cols, chunk, index, query_g, key_g, cosine, sine):
    heads, kv, group, keys, head_in, head, lse, gain, query_table, of_keys = attn_specs(
        raw, q_cols, kv_cols, chunk, index
    )
    key_in, value_in, key_table, _ = of_keys(keys)
    return pl.pallas_call(
        functools.partial(attn_fwd_kernel, min(256, chunk)),
        grid=(kv, group),
        in_specs=[head_in, key_in, value_in, gain, gain, query_table, query_table, key_table, key_table],
        out_specs=[head, lse],
        out_shape=[
            jax.ShapeDtypeStruct((chunk, heads * HD), BF),
            jax.ShapeDtypeStruct((heads, 1, chunk), F32),
        ],
        scratch_shapes=[
            pltpu.VMEM((chunk, HD), BF),
            pltpu.VMEM((keys, HD), BF),
            pltpu.VMEM((HD, keys), BF),
            pltpu.VMEM((keys, chunk), BF),
        ],
        compiler_params=params(40),
    )(raw, raw, raw, query_g, key_g, cosine, sine, cosine, sine)


def attn_bwd_kernel(
    block, keys, first, last, q_ref, k_ref, v_ref, ctx_ref, grad_ref, lse_ref, qg_ref, kg_ref,
    qcos_ref, qsin_ref, kcos_ref, ksin_ref, *rest,
):
    if first:
        dq_ref, dk_ref, dv_ref, dqg_ref, dkg_ref, qs, ks, kt, vs, ps, ds, dks, dvs = rest
    else:
        (dk_in, dv_in, dqg_in, dq_ref, dk_ref, dv_ref, dqg_ref, dkg_ref,
         qs, ks, kt, vs, ps, ds, dks, dvs) = rest
    chunk = q_ref.shape[0]
    base = (keys - chunk) // block
    kv_id, g_id = pl.program_id(0), pl.program_id(1)

    @pl.when(g_id == 0)
    def _():
        rotated = head_norm(k_ref[:keys], kg_ref[...], kcos_ref[:keys], ksin_ref[:keys]).astype(BF)
        ks[...] = rotated
        kt[...] = rotated.T
        vs[...] = v_ref[:keys].astype(BF)
        dks[...] = jnp.zeros_like(dks) if first else dk_in[...]
        dvs[...] = jnp.zeros_like(dvs) if first else dv_in[...]

    @pl.when((g_id == 0) & (kv_id == 0))
    def _():
        dqg_ref[...] = jnp.zeros_like(dqg_ref) if first else dqg_in[...]
        dkg_ref[...] = jnp.zeros_like(dkg_ref)

    qs[...] = head_norm(q_ref[...], qg_ref[...], qcos_ref[...], qsin_ref[...]).astype(BF)
    mask = causal_mask(block)
    for i in range(chunk // block):
        cols = slice(i * block, (i + 1) * block)
        product = grad_ref[cols].astype(F32) * ctx_ref[cols].astype(F32)
        delta = jnp.sum(product.T, axis=0, keepdims=True)
        lse = lse_ref[0, :, cols]
        for j in range(base + i + 1):
            rows = slice(j * block, (j + 1) * block)
            probs = jnp.exp2(dot_nt(ks[rows], qs[cols]) * (SCALE * LOG2E) - lse)
            if j == base + i:
                probs = jnp.where(mask, probs, 0.0)
            grad_probs = dot_nt(vs[rows], grad_ref[cols])
            ps[rows, cols] = probs.astype(BF)
            ds[rows, cols] = (probs * (grad_probs - delta)).astype(BF)
    for j in range(keys // block):
        rows = slice(j * block, (j + 1) * block)
        start = max(0, j - base) * block
        dvs[rows] += dot(ps[rows, start:], grad_ref[start:])
        dks[rows] += dot(ds[rows, start:], qs[start:])
    gain_sum = jnp.zeros((1, HD), F32)
    for i in range(chunk // block):
        cols = slice(i * block, (i + 1) * block)
        end = (base + i + 1) * block
        grad_t = dot(kt[:, :end], ds[:end, cols])
        grad_raw, part = head_norm_back(q_ref[cols], qg_ref[...], qcos_ref[cols], qsin_ref[cols], grad_t.T * SCALE)
        dq_ref[cols] = grad_raw.astype(BF)
        gain_sum = gain_sum + part
    dqg_ref[...] += gain_sum

    @pl.when(g_id == pl.num_programs(1) - 1)
    def _():
        if last:
            grad_raw, part = head_norm_back(k_ref[...], kg_ref[...], kcos_ref[...], ksin_ref[...], dks[...] * SCALE)
            dk_ref[...] = grad_raw.astype(BF)
            dv_ref[...] = dvs[...].astype(BF)
            dkg_ref[...] += part
        else:
            dk_ref[...] = dks[...]
            dv_ref[...] = dvs[...]


def attention_bwd(
    raw, q_cols, kv_cols, chunk, index, context, grad_context, lse_rows, query_g, key_g, cosine, sine, earlier, last
):
    seq = raw.shape[0]
    heads, kv, group, keys, head_in, head, lse, gain, query_table, of_keys = attn_specs(
        raw, q_cols, kv_cols, chunk, index
    )
    key_in, value_in, key_table, key_out = of_keys(seq)
    first = earlier is None
    more = [] if first else list(earlier)
    kind = BF if last else F32
    return pl.pallas_call(
        functools.partial(attn_bwd_kernel, min(256, chunk), keys, first, last),
        grid=(kv, group),
        in_specs=[head_in, key_in, value_in, head, head, lse, gain, gain, query_table, query_table, key_table, key_table]
        + ([] if first else [key_out, key_out, gain]),
        out_specs=[head, key_out, key_out, gain, gain],
        out_shape=[
            jax.ShapeDtypeStruct((chunk, heads * HD), BF),
            jax.ShapeDtypeStruct((seq, kv * HD), kind),
            jax.ShapeDtypeStruct((seq, kv * HD), kind),
            jax.ShapeDtypeStruct((1, HD), F32),
            jax.ShapeDtypeStruct((1, HD), F32),
        ],
        scratch_shapes=[
            pltpu.VMEM((chunk, HD), BF),
            pltpu.VMEM((keys, HD), BF),
            pltpu.VMEM((HD, keys), BF),
            pltpu.VMEM((keys, HD), BF),
            pltpu.VMEM((keys, chunk), BF),
            pltpu.VMEM((keys, chunk), BF),
            pltpu.VMEM((seq, HD), F32),
            pltpu.VMEM((seq, HD), F32),
        ],
        compiler_params=params(48),
    )(raw, raw, raw, context, grad_context, lse_rows, query_g, key_g, cosine, sine, cosine, sine, *more)


def rope_tables(seq):
    position = lax.iota(F32, seq)
    freq = THETA ** (-2.0 * lax.iota(F32, HD // 2) / HD)
    angle = position[:, None] * freq[None, :]
    cosine, sine = jnp.cos(angle), jnp.sin(angle)
    return jnp.concatenate([cosine, cosine], axis=1), jnp.concatenate([-sine, sine], axis=1)


def bits_of(count):
    return count.bit_length() - 1


def swap(value, bit):
    count = lax.axis_size("dp")
    return lax.ppermute(value, "dp", [(i, i ^ (1 << bit)) for i in range(count)])


def swap_pair(value):
    return lax.ppermute(value, "tensor", [(0, 1), (1, 0)])


def after(value, *needed):
    return lax.optimization_barrier((value, needed))[0]


def block_order():
    count = lax.axis_size("dp")
    bits = bits_of(count)
    reverse = np.array([int(format(i, "b").zfill(bits)[::-1], 2) if bits else 0 for i in range(count)], np.int32)
    return jnp.asarray(reverse) ^ lax.axis_index("dp").astype(jnp.int32)


def join_kernel(count, turn_ref, order_ref, one_ref, two_ref, out_ref):
    block = out_ref.shape[1] // count

    def fill(ref):
        for i in range(count):
            column = pl.multiple_of(order_ref[i] * block, block)
            out_ref[:, i * block : (i + 1) * block] = ref[:, pl.ds(column, block)]

    @pl.when(pl.program_id(0) == turn_ref[0])
    def _():
        fill(one_ref)

    @pl.when(pl.program_id(0) != turn_ref[0])
    def _():
        fill(two_ref)


def join(one, two, turn, order):
    rows, width = one.shape
    count = order.shape[0]
    tile = min(256, rows)
    turn = jnp.asarray(turn, jnp.int32)
    if (width // count) % 128:
        both = jnp.where(turn == 0, jnp.concatenate([one, two], axis=0), jnp.concatenate([two, one], axis=0))
        return jnp.take(both.reshape(2 * rows, count, -1), order, axis=1).reshape(2 * rows, width)
    steps = rows // tile
    half = pl.BlockSpec((tile, width), lambda h, r: (r, 0))
    return pl.pallas_call(
        functools.partial(join_kernel, count),
        grid=(2, steps),
        in_specs=[pl.BlockSpec(memory_space=pltpu.SMEM), pl.BlockSpec(memory_space=pltpu.SMEM), half, half],
        out_specs=pl.BlockSpec((tile, width), lambda h, r: (h * steps + r, 0)),
        out_shape=jax.ShapeDtypeStruct((2 * rows, width), one.dtype),
        compiler_params=params(32),
    )(turn.reshape(1), order, one, two)


def pick(turn_ref, index, own_ref, other_ref):
    return jnp.where(turn_ref[0] == index, own_ref[...].astype(F32), other_ref[...].astype(F32))


def mean_square(values):
    return lax.rsqrt(jnp.mean(values * values, axis=-1, keepdims=True) + EPS)


def mid_kernel(index, turn_ref, own_ref, other_ref, part_ref, got_ref, gain_ref, mid_ref, normed_ref):
    mid = pick(turn_ref, index, own_ref, other_ref) + (part_ref[...].astype(F32) + got_ref[...].astype(F32))
    mid_ref[...] = mid
    normed_ref[...] = (mid * mean_square(mid) * gain_ref[...]).astype(BF)


def middle(own, other, part, got, gain, turn, index):
    rows, width = own.shape
    tile = min(128, rows)
    block = pl.BlockSpec((tile, width), lambda r: (r, 0))
    return pl.pallas_call(
        functools.partial(mid_kernel, index),
        grid=(rows // tile,),
        in_specs=[pl.BlockSpec(memory_space=pltpu.SMEM)] + [block] * 4 + [pl.BlockSpec((1, width), lambda r: (0, 0))],
        out_specs=[block, block],
        out_shape=[jax.ShapeDtypeStruct((rows, width), F32), jax.ShapeDtypeStruct((rows, width), BF)],
        compiler_params=params(32),
    )(turn.reshape(1), own, other, part, got, gain)


def norm_back(values, gain, grad):
    scale = mean_square(values)
    scaled = grad * gain
    inner = jnp.mean(scaled * values, axis=-1, keepdims=True)
    grad_values = scale * scaled - values * (scale * scale * scale) * inner
    return grad_values, jnp.sum(grad * values * scale, axis=0, keepdims=True)


def mid_back_kernel(index, turn_ref, own_ref, other_ref, part_ref, got_ref, mid_ref, gain_ref, out_ref, low_ref, sum_ref):
    grad = part_ref[...].astype(F32) + got_ref[...].astype(F32)
    back, part = norm_back(mid_ref[...], gain_ref[...], grad)
    total = pick(turn_ref, index, own_ref, other_ref) + back
    out_ref[...] = total
    low_ref[...] = total.astype(BF)

    @pl.when(pl.program_id(0) == 0)
    def _():
        sum_ref[...] = jnp.zeros_like(sum_ref)

    sum_ref[...] += part


def middle_back(own, other, part, got, mid, gain, turn, index):
    rows, width = own.shape
    tile = min(128, rows)
    block = pl.BlockSpec((tile, width), lambda r: (r, 0))
    line = pl.BlockSpec((1, width), lambda r: (0, 0))
    return pl.pallas_call(
        functools.partial(mid_back_kernel, index),
        grid=(rows // tile,),
        in_specs=[pl.BlockSpec(memory_space=pltpu.SMEM)] + [block] * 5 + [line],
        out_specs=[block, block, line],
        out_shape=[
            jax.ShapeDtypeStruct((rows, width), F32),
            jax.ShapeDtypeStruct((rows, width), BF),
            jax.ShapeDtypeStruct((1, width), F32),
        ],
        compiler_params=params(32),
    )(turn.reshape(1), own, other, part, got, mid, gain)


def expert_kernel(x_ref, own_ref, other_ref, turn_ref, gate_ref, up_ref, down_ref, route_ref, weight_ref, *rest, index):
    hidden_ref, gg_ref, gu_ref = rest[-3:]
    expert = pl.program_id(0)
    share = jnp.sum(jnp.where(route_ref[...] == expert, weight_ref[...], 0.0), axis=-1, keepdims=True)
    gate = dot(x_ref[...], gate_ref[...])
    up = dot(x_ref[...], up_ref[...])
    cot = jnp.where(turn_ref[0] == index, own_ref[...], other_ref[...])
    grad_hidden = dot(cot, down_ref[...]) * share
    sigma = 1.0 / (1.0 + jnp.exp(-gate))
    silu = gate * sigma
    hidden_ref[...] = (silu * up * share).astype(BF)
    gg_ref[...] = (grad_hidden * up * sigma * (1.0 + gate * (1.0 - sigma))).astype(BF)
    gu_ref[...] = (grad_hidden * silu).astype(BF)


def expert_part(normed, own, other, weights, routes, route_weights, turn, index, experts, earlier):
    rows, width = normed.shape
    cols = weights.shape[1] // (3 * experts)
    seq = routes.shape[0]
    full = pl.BlockSpec((rows, width), lambda e: (0, 0))
    scalar = pl.BlockSpec(memory_space=pltpu.SMEM)
    pair = pl.BlockSpec((rows, routes.shape[1]), lambda e: (index, 0))
    out = pl.BlockSpec((rows, cols), lambda e: (index, e))
    more = [] if earlier is None else list(earlier)
    return pl.pallas_call(
        functools.partial(expert_kernel, index=index),
        grid=(experts,),
        in_specs=[full, full, full, scalar]
        + [pl.BlockSpec((width, cols), lambda e, k=k: (0, k * experts + e)) for k in range(3)]
        + [pair, pair]
        + [pl.BlockSpec(memory_space=pl.ANY)] * len(more),
        out_specs=[out, out, out],
        out_shape=[jax.ShapeDtypeStruct((seq, experts * cols), BF)] * 3,
        input_output_aliases={9 + i: i for i in range(len(more))},
        compiler_params=params(56),
    )(normed, own, other, turn.reshape(1), weights, weights, weights, routes, route_weights, *more)


def fold(keep, received):
    return (keep.astype(F32) + received.astype(F32)).astype(BF)


def sum_all(value):
    for bit in range(bits_of(lax.axis_size("dp"))):
        value = value + swap(value, bit)
    return value + swap_pair(value)


class Reduction:
    def __init__(self, left, right, order, *needed):
        self.order = list(order)
        self.block = left.shape[1] // lax.axis_size("dp")
        half = left.shape[1] // 2
        self.left, self.right = left[:, :half], right
        self.sent = dot_tn(after(left[:, half:], *needed), right).astype(BF)
        self.got = swap(self.sent, 0)

    def keep(self, *needed):
        total = dot_tn(after(self.left, *needed), self.right) + self.got.astype(F32)
        self.axes = list(range(1, bits_of(lax.axis_size("dp"))))
        shape = (2,) * len(self.axes) + (self.block, total.shape[1])
        self.held = total.astype(BF).reshape(shape)
        self.send()
        return self.held

    def send(self):
        axis = self.axes.index(self.order[0])
        self.mine = lax.index_in_dim(self.held, 0, axis, keepdims=False)
        self.got = swap(lax.index_in_dim(self.held, 1, axis, keepdims=False), self.order[0])

    def step(self, *needed):
        self.axes.remove(self.order.pop(0))
        mine = after(self.mine, *needed) if needed else self.mine
        if not self.order:
            return mine.astype(F32) + self.got.astype(F32)
        self.held = fold(mine, self.got)
        self.send()
        return self.held

    def finish(self, *needed):
        while True:
            result = self.step(*needed)
            if not self.order:
                return result


def body(
    tokens, cotangent, routes, route_weights, query_weight, key_weight, value_weight, out_weight,
    gate_weight, up_weight, down_weight, attn_gain, ffn_gain, query_gain, key_gain,
):
    turn = lax.axis_index("tensor").astype(jnp.int32)
    chunk = tokens.shape[0]
    seq = 2 * chunk
    width = tokens.shape[1]
    order = block_order()
    cosine, sine = rope_tables(seq)
    experts, hidden_cols = gate_weight.shape[2], gate_weight.shape[3]
    flat = experts * hidden_cols
    q_cols, kv_cols = query_weight.shape[2], key_weight.shape[2]
    qkv_cols = q_cols + 2 * kv_cols
    bits = bits_of(lax.axis_size("dp"))
    straight = list(range(1, bits))
    crossed = straight if bits < 3 else [2, 1] + straight[2:]
    row_routes, row_weights = routes[0], route_weights[0]

    def select(zero, one):
        return jnp.where(turn == 0, zero, one)

    attn_w = lax.all_gather(
        jnp.concatenate([query_weight[0], key_weight[0], value_weight[0], out_weight[0]], axis=1),
        "dp", axis=0, tiled=True,
    )
    ffn_w = lax.all_gather(
        jnp.concatenate([w[0].reshape(-1, flat) for w in (gate_weight, up_weight, down_weight)], axis=1),
        "dp", axis=0, tiled=True,
    )
    qkv_w, out_w = attn_w[:, :qkv_cols], attn_w[:, qkv_cols:]
    gate_up_w, down_w = ffn_w[:, : 2 * flat], ffn_w[:, 2 * flat :]

    tokens_other = swap_pair(tokens)
    cot_other = swap_pair(cotangent)
    resid = select(
        jnp.concatenate([tokens, tokens_other], axis=0), jnp.concatenate([tokens_other, tokens], axis=0)
    ).astype(F32)
    normed = (resid * mean_square(resid) * attn_gain).astype(BF)
    normed_rel = join(normed[:chunk], normed[chunk:], 0, order)
    cot_rel = join(cotangent, cot_other, turn, order)

    raw = dot(after(normed, normed_rel, cot_rel), qkv_w)
    context, lse, part, got = {}, {}, {}, {}
    last = raw
    for index in (1, 0):
        context[index], lse[index] = attention_fwd(
            after(raw, last), q_cols, kv_cols, chunk, index, query_gain, key_gain, cosine, sine
        )
        part[index] = dot_nt(context[index], out_w).astype(BF)
        got[index] = swap_pair(part[index])
        last = part[index]

    mid, normed_f, back_part, back_got = {}, {}, {}, {}
    done = None
    for index in (1, 0):
        mid[index], normed_f[index] = middle(
            tokens, tokens_other, after(part[index], last), got[index], ffn_gain, turn, index
        )
        done = expert_part(
            normed_f[index], cotangent, cot_other, ffn_w, row_routes, row_weights, turn, index, experts, done
        )
        rows = slice(index * chunk, (index + 1) * chunk)
        grad_gate_up = jnp.concatenate([done[1][rows], done[2][rows]], axis=1)
        back_part[index] = dot_nt(grad_gate_up, gate_up_w).astype(BF)
        back_got[index] = swap_pair(back_part[index])
        last = back_part[index]
        done = [after(value, last) for value in done]
    hidden, grad_gate, grad_up = done
    normed_f_rel = join(after(normed_f[0], last), normed_f[1], 0, order)

    down_sum = Reduction(cot_rel, hidden, straight, normed_f_rel)
    gate_sum = Reduction(normed_f_rel, grad_gate, straight, down_sum.sent)
    up_sum = Reduction(normed_f_rel, grad_up, crossed, gate_sum.sent)
    last = down_sum.keep(up_sum.sent)
    last = up_sum.keep(last)
    last = gate_sum.keep(last)

    grad_mid, grad_mid_b, ffn_parts, grad_context, dq = {}, {}, {}, {}, {}
    earlier = None
    for index in (1, 0):
        grad_mid[index], grad_mid_b[index], ffn_parts[index] = middle_back(
            cotangent, cot_other, after(back_part[index], last), back_got[index], mid[index], ffn_gain, turn, index
        )
        grad_context[index] = dot(grad_mid_b[index], out_w).astype(BF)
        if index == 0:
            grad_mid_rel = join(after(grad_mid_b[0], grad_context[0]), grad_mid_b[1], 0, order)
            all_context = jnp.concatenate([context[0], context[1]], axis=0)
            out_sum = Reduction(grad_mid_rel, all_context, straight)
            last = out_sum.sent
            last = out_sum.keep(last)
            last = down_sum.step(last)
            last = up_sum.step(last)
        dq[index], dk, dv, query_part, key_part = attention_bwd(
            raw, q_cols, kv_cols, chunk, index, context[index], after(grad_context[index], last), lse[index],
            query_gain, key_gain, cosine, sine, earlier, index == 0,
        )
        earlier = (dk, dv, query_part)
        last = dq[index]
        if index == 1:
            hidden_theirs = select(hidden[chunk:], hidden[:chunk])
            out_theirs = dot_nt(after(hidden_theirs, last), down_w).astype(BF)
            hidden_mine = select(hidden[:chunk], hidden[chunk:])
            out_mine = dot_nt(after(hidden_mine, out_theirs), down_w).astype(BF)
            last = out_mine

    last = gate_sum.step(last)
    last = down_sum.step(last)
    theirs = jnp.concatenate([select(dq[1], dq[0]), select(dk[chunk:], dk[:chunk]), select(dv[chunk:], dv[:chunk])], axis=1)
    grad_theirs = dot_nt(after(theirs, last), qkv_w).astype(BF)
    grad_qkv = jnp.concatenate([jnp.concatenate([dq[0], dq[1]], axis=0), dk, dv], axis=1)
    grad_got = swap_pair(grad_theirs)
    middle_col = qkv_cols // 2
    one_sum = Reduction(normed_rel, grad_qkv[:, :middle_col], crossed, grad_theirs)
    two_sum = Reduction(normed_rel, grad_qkv[:, middle_col:], straight, one_sum.sent)
    last = up_sum.step(two_sum.sent)
    last = out_sum.step(last)
    last = one_sum.keep(last)
    last = two_sum.keep(last)
    mine = select(grad_qkv[:chunk], grad_qkv[chunk:])
    grad_mine = dot_nt(after(mine, last), qkv_w)
    down_grad = down_sum.finish(grad_mine)
    last = gate_sum.step(down_grad)
    last = one_sum.step(last)
    last = out_sum.step(last)
    output = select(mid[0], mid[1]) + (out_mine.astype(F32) + swap_pair(after(out_theirs, grad_theirs)).astype(F32))
    output = after(output, last).astype(BF)
    last = two_sum.step(output)
    up_grad = up_sum.finish(last)
    gate_grad = gate_sum.finish(up_grad)
    last = one_sum.step(gate_grad)
    last = two_sum.step(last)

    grad_normed = after(grad_mine, last) + grad_got.astype(F32)
    grad_one, attn_part = norm_back(tokens.astype(F32), attn_gain, grad_normed)
    tokens_grad = select(grad_mid[0], grad_mid[1]) + grad_one
    out_grad = out_sum.finish(tokens_grad)
    ffn_part = (ffn_parts[0] + ffn_parts[1]) * 0.5
    small = sum_all(jnp.concatenate([attn_part, ffn_part, query_part, key_part], axis=1))
    one_grad = one_sum.finish(out_grad)
    two_grad = two_sum.finish(one_grad)
    qkv_grad = jnp.concatenate([one_grad, two_grad], axis=1)

    def expert(values):
        return values.reshape(1, -1, experts, hidden_cols)

    return (
        output,
        tokens_grad,
        qkv_grad[None, :, :q_cols],
        qkv_grad[None, :, q_cols : q_cols + kv_cols],
        qkv_grad[None, :, q_cols + kv_cols :],
        out_grad[None],
        expert(gate_grad),
        expert(up_grad),
        expert(down_grad),
        small[:, :width],
        small[:, width : 2 * width],
        small[:, 2 * width : 2 * width + HD],
        small[:, 2 * width + HD :],
    )


def solution(mesh):
    return jax.shard_map(
        body,
        mesh=mesh,
        in_specs=(
            P(("dp", "tensor"), None),
            P(("dp", "tensor"), None),
            P(None, "dp", None),
            P(None, "dp", None),
            P(None, "dp", "tensor"),
            P(None, "dp", "tensor"),
            P(None, "dp", "tensor"),
            P(None, "dp", "tensor"),
            P(None, "dp", None, "tensor"),
            P(None, "dp", None, "tensor"),
            P(None, "dp", None, "tensor"),
            P(),
            P(),
            P(),
            P(),
        ),
        out_specs=(
            P(("dp", "tensor"), None),
            P(("dp", "tensor"), None),
            P(None, "dp", "tensor"),
            P(None, "dp", "tensor"),
            P(None, "dp", "tensor"),
            P(None, "dp", "tensor"),
            P(None, "dp", None, "tensor"),
            P(None, "dp", None, "tensor"),
            P(None, "dp", None, "tensor"),
            P(),
            P(),
            P(),
            P(),
        ),
        check_vma=False,
    )
```

```python
import functools
import math

import jax
import jax.numpy as jnp
import numpy as np
from jax import lax
from jax.experimental import pallas as pl
from jax.experimental.pallas import tpu as pltpu
from jax.sharding import PartitionSpec as P

HD = 128
EPS = 1e-06
THETA = 1000000.0
SCALE = HD ** -0.5
LOG2E = math.log2(math.e)
NT = (((1,), (1,)), ((), ()))
BF = jnp.bfloat16
F32 = jnp.float32


def params(mib):
    return pltpu.CompilerParams(vmem_limit_bytes=mib * 2**20)


def dot(left, right):
    return jnp.dot(left, right, preferred_element_type=F32)


def dot_nt(left, right):
    return lax.dot_general(left, right, NT, preferred_element_type=F32)


def dot_tn(left, right):
    return lax.dot_general(left, right, (((0,), (0,)), ((), ())), preferred_element_type=F32)


def head_norm(values, gain, cosine, sine):
    scale = lax.rsqrt(jnp.mean(values * values, axis=-1, keepdims=True) + EPS)
    normed = values * scale * gain
    return normed * cosine + pltpu.roll(normed, HD // 2, 1) * sine


def head_norm_back(values, gain, cosine, sine, grad_rot):
    scale = lax.rsqrt(jnp.mean(values * values, axis=-1, keepdims=True) + EPS)
    grad = grad_rot * cosine - pltpu.roll(grad_rot, HD // 2, 1) * sine
    scaled = grad * gain
    inner = jnp.mean(scaled * values, axis=-1, keepdims=True)
    grad_values = scale * scaled - values * (scale * scale * scale) * inner
    return grad_values, jnp.sum(grad * values * scale, axis=0, keepdims=True)


def causal(offset, rows, columns):
    key = lax.broadcasted_iota(jnp.int32, (rows, columns), 0) + offset
    return key <= lax.broadcasted_iota(jnp.int32, (rows, columns), 1)


def attn_fwd_kernel(block, q_ref, k_ref, v_ref, qg_ref, kg_ref, qcos_ref, qsin_ref, kcos_ref, ksin_ref, *rest):
    out_ref, lse_ref, qs, ks, vt, ps, ss, mix, sums = rest[-9:]
    chunk, per = q_ref.shape[0], q_ref.shape[1] // HD
    base = k_ref.shape[0] - chunk
    tile = min(64, block)

    @pl.when(pl.program_id(1) == 0)
    def _():
        ks[...] = head_norm(k_ref[...], kg_ref[...], kcos_ref[...], ksin_ref[...]).astype(BF)
        vt[...] = v_ref[...].astype(BF).T

    for h in range(per):
        lanes = slice(h * HD, (h + 1) * HD)
        qs[h] = head_norm(q_ref[:, lanes], qg_ref[...], qcos_ref[...], qsin_ref[...]).astype(BF)
    pairs = [(h, i) for h in range(per) for i in range(chunk // block)]

    def place(h, i):
        start = base + i * block
        return slice(h * HD, (h + 1) * HD), slice(i * block, (i + 1) * block), start, start + block

    for h, i in pairs:
        lanes, cols, start, end = place(h, i)
        ss[h, :end, cols] = dot_nt(ks[:end], qs[h, cols])
    for h, i in pairs:
        lanes, cols, start, end = place(h, i)
        total = jnp.zeros((8, block), F32)
        for r in range(0, end, tile):
            probs = jnp.exp2(ss[h, r : r + tile, cols] * (SCALE * LOG2E))
            if r >= start:
                probs = jnp.where(causal(r - start, tile, block), probs, 0.0)
            total = total + jnp.sum(probs.reshape(tile // 8, 8, block), axis=0)
            ps[h, r : r + tile, cols] = probs.astype(BF)
        sums[h, :, cols] = jnp.sum(total, axis=0, keepdims=True)
    for h, i in pairs:
        lanes, cols, start, end = place(h, i)
        mix[h, :, cols] = dot(vt[:, :end], ps[h, :end, cols])
    for h, i in pairs:
        lanes, cols, start, end = place(h, i)
        out_ref[cols, lanes] = (mix[h, :, cols] * (1.0 / sums[h, :, cols])).T.astype(BF)
    lse_ref[...] = jnp.log2(sums[...])


def attn_specs(raw, q_cols, kv_cols, chunk, index, per):
    heads, kv = q_cols // HD, kv_cols // HD
    steps = heads // kv // per
    keys = (index + 1) * chunk
    head_in = pl.BlockSpec((chunk, per * HD), lambda k, g: (index, k * steps + g))
    head = pl.BlockSpec((chunk, per * HD), lambda k, g: (0, k * steps + g))
    lse = pl.BlockSpec((per, 1, chunk), lambda k, g: (k * steps + g, 0, 0))
    gain = pl.BlockSpec((1, HD), lambda k, g: (0, 0))
    query_table = pl.BlockSpec((chunk, HD), lambda k, g: (index, 0))

    def of_keys(rows):
        return (
            pl.BlockSpec((rows, HD), lambda k, g: (0, heads + k)),
            pl.BlockSpec((rows, HD), lambda k, g: (0, heads + kv + k)),
            pl.BlockSpec((rows, HD), lambda k, g: (0, 0)),
            pl.BlockSpec((rows, HD), lambda k, g: (0, k)),
        )

    return heads, kv, steps, keys, head_in, head, lse, gain, query_table, of_keys


def attention_fwd(raw, q_cols, kv_cols, chunk, index, query_g, key_g, cosine, sine, earlier):
    seq = raw.shape[0]
    more = [] if earlier is None else [earlier]
    per = min(4, q_cols // kv_cols)
    heads, kv, steps, keys, head_in, head, lse, gain, query_table, of_keys = attn_specs(
        raw, q_cols, kv_cols, chunk, index, per
    )
    key_in, value_in, key_table, _ = of_keys(keys)
    return pl.pallas_call(
        functools.partial(attn_fwd_kernel, min(256, chunk)),
        grid=(kv, steps),
        in_specs=[head_in, key_in, value_in, gain, gain, query_table, query_table, key_table, key_table]
        + [pl.BlockSpec(memory_space=pl.ANY)] * len(more),
        out_specs=[head_in, lse],
        out_shape=[
            pltpu.HBM((seq, heads * HD), BF),
            jax.ShapeDtypeStruct((heads, 1, chunk), F32),
        ],
        scratch_shapes=[
            pltpu.VMEM((per, chunk, HD), BF),
            pltpu.VMEM((keys, HD), BF),
            pltpu.VMEM((HD, keys), BF),
            pltpu.VMEM((per, keys, chunk), BF),
            pltpu.VMEM((per, keys, chunk), F32),
            pltpu.VMEM((per, HD, chunk), F32),
            pltpu.VMEM((per, 1, chunk), F32),
        ],
        input_output_aliases={9: 0} if more else {},
        compiler_params=params(48),
    )(raw, raw, raw, query_g, key_g, cosine, sine, cosine, sine, *more)


def attn_bwd_kernel(
    block, keys, first, last, q_ref, k_ref, v_ref, ctx_ref, grad_ref, lse_ref, qg_ref, kg_ref,
    qcos_ref, qsin_ref, kcos_ref, ksin_ref, *rest,
):
    if first:
        dq_ref, dk_ref, dv_ref, dqg_ref, dkg_ref, qs, ks, kt, vs, ps, ds, dks, dvs, ss, gs, deltas, dqs = rest
    else:
        (dk_in, dv_in, dqg_in, dq_in, dq_ref, dk_ref, dv_ref, dqg_ref, dkg_ref,
         qs, ks, kt, vs, ps, ds, dks, dvs, ss, gs, deltas, dqs) = rest
    chunk, per = q_ref.shape[0], q_ref.shape[1] // HD
    base = (keys - chunk) // block
    kv_id, g_id = pl.program_id(0), pl.program_id(1)

    @pl.when(g_id == 0)
    def _():
        rotated = head_norm(k_ref[:keys], kg_ref[...], kcos_ref[:keys], ksin_ref[:keys]).astype(BF)
        ks[...] = rotated
        kt[...] = rotated.T
        vs[...] = v_ref[:keys].astype(BF)
        dks[...] = jnp.zeros_like(dks) if first else dk_in[...]
        dvs[...] = jnp.zeros_like(dvs) if first else dv_in[...]

    @pl.when((g_id == 0) & (kv_id == 0))
    def _():
        dqg_ref[...] = jnp.zeros_like(dqg_ref) if first else dqg_in[...]
        dkg_ref[...] = jnp.zeros_like(dkg_ref)

    tile = min(64, block)
    for h in range(per):
        lanes = slice(h * HD, (h + 1) * HD)
        qs[h] = head_norm(q_ref[:, lanes], qg_ref[...], qcos_ref[...], qsin_ref[...]).astype(BF)
    pairs = [(h, i) for h in range(per) for i in range(chunk // block)]

    def place(h, i):
        start = (base + i) * block
        return slice(h * HD, (h + 1) * HD), slice(i * block, (i + 1) * block), start, start + block

    def first_products(h):
        for i in range(chunk // block):
            lanes, cols, start, end = place(h, i)
            product = grad_ref[cols, lanes].astype(F32) * ctx_ref[cols, lanes].astype(F32)
            deltas[h, :, cols] = jnp.sum(product.T, axis=0, keepdims=True)
            ss[h % 2, :end, cols] = dot_nt(ks[:end], qs[h, cols])
            gs[h % 2, :end, cols] = dot_nt(vs[:end], grad_ref[cols, lanes])

    def weights(h):
        for i in range(chunk // block):
            lanes, cols, start, end = place(h, i)
            delta, lse = deltas[h, :, cols], lse_ref[h, :, cols]
            for r in range(0, end, tile):
                rows = slice(r, r + tile)
                probs = jnp.exp2(ss[h % 2, rows, cols] * (SCALE * LOG2E) - lse)
                if r >= start:
                    probs = jnp.where(causal(r - start, tile, block), probs, 0.0)
                ps[h % 2, rows, cols] = probs.astype(BF)
                ds[h % 2, rows, cols] = (probs * (gs[h % 2, rows, cols] - delta)).astype(BF)

    def second_products(h):
        lanes = slice(h * HD, (h + 1) * HD)
        for j in range(keys // block):
            rows = slice(j * block, (j + 1) * block)
            start = max(0, j - base) * block
            dvs[rows] += dot(ps[h % 2, rows, start:], grad_ref[start:, lanes])
            dks[rows] += dot(ds[h % 2, rows, start:], qs[h, start:])
        for i in range(chunk // block):
            lanes, cols, start, end = place(h, i)
            dqs[h % 2, :, cols] = dot(kt[:, :end], ds[h % 2, :end, cols])

    def last_part(h):
        total = jnp.zeros((1, HD), F32)
        for i in range(chunk // block):
            lanes, cols, start, end = place(h, i)
            grad_raw, part = head_norm_back(
                q_ref[cols, lanes], qg_ref[...], qcos_ref[cols], qsin_ref[cols], dqs[h % 2, :, cols].T * SCALE
            )
            dq_ref[cols, lanes] = grad_raw.astype(BF)
            total = total + part
        return total

    gain_sum = jnp.zeros((1, HD), F32)
    first_products(0)
    for h in range(per):
        if h + 1 < per:
            first_products(h + 1)
        weights(h)
        if h:
            gain_sum = gain_sum + last_part(h - 1)
        second_products(h)
    gain_sum = gain_sum + last_part(per - 1)
    dqg_ref[...] += gain_sum

    @pl.when(g_id == pl.num_programs(1) - 1)
    def _():
        if last:
            grad_raw, part = head_norm_back(k_ref[...], kg_ref[...], kcos_ref[...], ksin_ref[...], dks[...] * SCALE)
            dk_ref[...] = grad_raw.astype(BF)
            dv_ref[...] = dvs[...].astype(BF)
            dkg_ref[...] += part
        else:
            dk_ref[...] = dks[...]
            dv_ref[...] = dvs[...]


def attention_bwd(
    raw, q_cols, kv_cols, chunk, index, context, grad_context, lse_rows, query_g, key_g, cosine, sine, earlier, last
):
    seq = raw.shape[0]
    per = min(4, q_cols // kv_cols)
    heads, kv, steps, keys, head_in, head, lse, gain, query_table, of_keys = attn_specs(
        raw, q_cols, kv_cols, chunk, index, per
    )
    key_in, value_in, key_table, key_out = of_keys(seq)
    first = earlier is None
    more = [] if first else list(earlier)
    kind = BF if last else F32
    return pl.pallas_call(
        functools.partial(attn_bwd_kernel, min(256, chunk), keys, first, last),
        grid=(kv, steps),
        in_specs=[head_in, key_in, value_in, head_in, head, lse, gain, gain, query_table, query_table, key_table, key_table]
        + ([] if first else [key_out, key_out, gain, pl.BlockSpec(memory_space=pl.ANY)]),
        out_specs=[head_in, key_out, key_out, gain, gain],
        out_shape=[
            jax.ShapeDtypeStruct((seq, heads * HD), BF),
            jax.ShapeDtypeStruct((seq, kv * HD), kind),
            jax.ShapeDtypeStruct((seq, kv * HD), kind),
            jax.ShapeDtypeStruct((1, HD), F32),
            jax.ShapeDtypeStruct((1, HD), F32),
        ],
        scratch_shapes=[
            pltpu.VMEM((per, chunk, HD), BF),
            pltpu.VMEM((keys, HD), BF),
            pltpu.VMEM((HD, keys), BF),
            pltpu.VMEM((keys, HD), BF),
            pltpu.VMEM((2, keys, chunk), BF),
            pltpu.VMEM((2, keys, chunk), BF),
            pltpu.VMEM((seq, HD), F32),
            pltpu.VMEM((seq, HD), F32),
            pltpu.VMEM((2, keys, chunk), F32),
            pltpu.VMEM((2, keys, chunk), F32),
            pltpu.VMEM((per, 1, chunk), F32),
            pltpu.VMEM((2, HD, chunk), F32),
        ],
        input_output_aliases={} if first else {15: 0},
        compiler_params=params(58),
    )(raw, raw, raw, in_hbm(context), grad_context, lse_rows, query_g, key_g, cosine, sine, cosine, sine, *more)


def rope_tables(seq):
    position = lax.iota(F32, seq)
    freq = THETA ** (-2.0 * lax.iota(F32, HD // 2) / HD)
    angle = position[:, None] * freq[None, :]
    cosine, sine = jnp.cos(angle), jnp.sin(angle)
    return jnp.concatenate([cosine, cosine], axis=1), jnp.concatenate([-sine, sine], axis=1)


def bits_of(count):
    return count.bit_length() - 1


def swap(value, bit):
    count = lax.axis_size("dp")
    return lax.ppermute(value, "dp", [(i, i ^ (1 << bit)) for i in range(count)])


def swap_pair(value):
    return lax.ppermute(value, "tensor", [(0, 1), (1, 0)])


def after(value, *needed):
    return lax.optimization_barrier((value, needed))[0]


def in_hbm(value):
    return pltpu.with_memory_space_constraint(value, pltpu.HBM)


def tie_kernel(*refs):
    pass


def tie(value, *needed):
    anywhere = pl.BlockSpec(memory_space=pl.ANY)
    return pl.pallas_call(
        tie_kernel,
        in_specs=[anywhere] * (1 + len(needed)),
        out_specs=anywhere,
        out_shape=jax.ShapeDtypeStruct(value.shape, value.dtype),
        input_output_aliases={0: 0},
    )(value, *needed)


def block_order():
    count = lax.axis_size("dp")
    bits = bits_of(count)
    reverse = np.array([int(format(i, "b").zfill(bits)[::-1], 2) if bits else 0 for i in range(count)], np.int32)
    return jnp.asarray(reverse) ^ lax.axis_index("dp").astype(jnp.int32)


def join_kernel(count, parts, turn_ref, order_ref, one_ref, two_ref, *out_refs):
    block = one_ref.shape[1] // count

    def fill(ref):
        for i in range(count):
            column = pl.multiple_of(order_ref[i] * block, block)
            out_ref, at = out_refs[i // (count // parts)], i % (count // parts)
            out_ref[:, at * block : (at + 1) * block] = ref[:, pl.ds(column, block)]

    @pl.when(pl.program_id(0) == turn_ref[0])
    def _():
        fill(one_ref)

    @pl.when(pl.program_id(0) != turn_ref[0])
    def _():
        fill(two_ref)


def join(one, two, turn, order, parts):
    rows, width = one.shape
    count = order.shape[0]
    tile = min(256, rows)
    turn = jnp.asarray(turn, jnp.int32)
    if (width // count) % 128:
        both = jnp.where(turn == 0, jnp.concatenate([one, two], axis=0), jnp.concatenate([two, one], axis=0))
        both = jnp.take(both.reshape(2 * rows, count, -1), order, axis=1).reshape(2 * rows, width)
        return jnp.split(both, parts, axis=1)
    steps = rows // tile
    half = pl.BlockSpec((tile, width), lambda h, r: (r, 0))
    scalar = pl.BlockSpec(memory_space=pltpu.SMEM)
    return pl.pallas_call(
        functools.partial(join_kernel, count, parts),
        grid=(2, steps),
        in_specs=[scalar, scalar, half, half],
        out_specs=[pl.BlockSpec((tile, width // parts), lambda h, r: (h * steps + r, 0))] * parts,
        out_shape=[jax.ShapeDtypeStruct((2 * rows, width // parts), one.dtype)] * parts,
        compiler_params=params(32),
    )(turn.reshape(1), order, one, two)


def mean_square(values):
    return lax.rsqrt(jnp.mean(values * values, axis=-1, keepdims=True) + EPS)


def mid_kernel(base_ref, part_ref, got_ref, gain_ref, *rest):
    mid_ref, normed_ref = rest[-2:]
    mid = base_ref[...].astype(F32) + (part_ref[...].astype(F32) + got_ref[...].astype(F32))
    mid_ref[...] = mid
    normed_ref[...] = (mid * mean_square(mid) * gain_ref[...]).astype(BF)


def middle(base, part, got, gain, index, earlier):
    rows, width = part.shape
    tile = min(128, rows)
    block = pl.BlockSpec((tile, width), lambda r: (r, 0))
    place = pl.BlockSpec((tile, width), lambda r: (index * (rows // tile) + r, 0))
    more = [] if earlier is None else [earlier]
    return pl.pallas_call(
        mid_kernel,
        grid=(rows // tile,),
        in_specs=[place, block, block, pl.BlockSpec((1, width), lambda r: (0, 0))]
        + [pl.BlockSpec(memory_space=pl.ANY)] * len(more),
        out_specs=[block, place],
        out_shape=[pltpu.HBM((rows, width), F32), pltpu.HBM(base.shape, BF)],
        input_output_aliases={4: 1} if more else {},
        compiler_params=params(32),
    )(base, part, got, gain, *more)


def norm_back(values, gain, grad):
    scale = mean_square(values)
    scaled = grad * gain
    inner = jnp.mean(scaled * values, axis=-1, keepdims=True)
    grad_values = scale * scaled - values * (scale * scale * scale) * inner
    return grad_values, jnp.sum(grad * values * scale, axis=0, keepdims=True)


def mid_back_kernel(base_ref, part_ref, got_ref, mid_ref, gain_ref, out_ref, low_ref, sum_ref):
    grad = part_ref[...].astype(F32) + got_ref[...].astype(F32)
    back, part = norm_back(mid_ref[...], gain_ref[...], grad)
    total = base_ref[...].astype(F32) + back
    out_ref[...] = total
    low_ref[...] = total.astype(BF)

    @pl.when(pl.program_id(0) == 0)
    def _():
        sum_ref[...] = jnp.zeros_like(sum_ref)

    sum_ref[...] += part


def middle_back(base, part, got, mid, gain, index):
    rows, width = part.shape
    tile = min(128, rows)
    block = pl.BlockSpec((tile, width), lambda r: (r, 0))
    line = pl.BlockSpec((1, width), lambda r: (0, 0))
    return pl.pallas_call(
        mid_back_kernel,
        grid=(rows // tile,),
        in_specs=[pl.BlockSpec((tile, width), lambda r: (index * (rows // tile) + r, 0)), block, block, block, line],
        out_specs=[block, block, line],
        out_shape=[
            pltpu.HBM((rows, width), F32),
            jax.ShapeDtypeStruct((rows, width), BF),
            jax.ShapeDtypeStruct((1, width), F32),
        ],
        compiler_params=params(32),
    )(base, part, got, in_hbm(mid), gain)


def expert_kernel(unit, cols, x_ref, cot_ref, gate_ref, up_ref, down_ref, route_ref, weight_ref, *rest):
    out_ref = rest[-1]
    step, count = pl.program_id(0), pl.num_programs(0)
    rows, block = x_ref.shape[0], gate_ref.shape[1]
    tile = min(256, rows)

    def place(kind):
        return pl.ds(pl.multiple_of((kind * count + step) * block, block), block)

    for r in range(rows // tile):
        part = slice(r * tile, (r + 1) * tile)
        shares = []
        for k in range(block // unit):
            expert = (step * (block // unit) + k) // (cols // unit)
            share = jnp.sum(jnp.where(route_ref[part] == expert, weight_ref[part], 0.0), axis=-1, keepdims=True)
            shares.append(jnp.broadcast_to(share, (tile, unit)))
        share = jnp.concatenate(shares, axis=1)
        gate = dot(x_ref[part], gate_ref[...])
        up = dot(x_ref[part], up_ref[...])
        grad_hidden = dot(cot_ref[part], down_ref[...]) * share
        sigma = 1.0 / (1.0 + jnp.exp(-gate))
        silu = gate * sigma
        out_ref[part, place(0)] = (grad_hidden * up * (sigma + silu * (1.0 - sigma))).astype(BF)
        out_ref[part, place(1)] = (grad_hidden * silu).astype(BF)
        out_ref[part, place(2)] = (silu * up * share).astype(BF)


def expert_part(normed, cot, weights, routes, route_weights, index, experts, earlier):
    width = normed.shape[1]
    flat = weights.shape[1] // 3
    cols = flat // experts
    unit = math.gcd(cols, 128)
    block = 2 * unit if flat % (2 * unit) == 0 else unit
    steps = flat // block
    seq = routes.shape[0]
    rows = seq // 2
    pair = pl.BlockSpec((rows, routes.shape[1]), lambda e: (index, 0))
    half = pl.BlockSpec((rows, width), lambda e: (index, 0))
    more = [] if earlier is None else [earlier]
    return pl.pallas_call(
        functools.partial(expert_kernel, unit, cols),
        grid=(steps,),
        in_specs=[half, half]
        + [pl.BlockSpec((width, block), lambda e, k=k: (0, k * steps + e)) for k in range(3)]
        + [pair, pair]
        + [pl.BlockSpec(memory_space=pl.ANY)] * len(more),
        out_specs=pl.BlockSpec((rows, 3 * flat), lambda e: (index, 0)),
        out_shape=jax.ShapeDtypeStruct((seq, 3 * flat), BF),
        input_output_aliases={7: 0} if more else {},
        compiler_params=params(56),
    )(in_hbm(normed), cot, weights, weights, weights, routes, route_weights, *more)


def expert_weight_kernel(cut, normed_ref, cot_ref, act_ref, out_ref):
    step = pl.program_id(0)

    @pl.when(step < cut)
    def _():
        out_ref[...] = dot_tn(normed_ref[...], act_ref[...]).astype(BF)

    @pl.when(step >= cut)
    def _():
        out_ref[...] = dot_tn(cot_ref[...], act_ref[...]).astype(BF)


def expert_weights(normed, cot, acts, block):
    seq, width = normed.shape
    flat = acts.shape[1] // 3
    full = pl.BlockSpec((seq, width), lambda j: (0, 0))
    return pl.pallas_call(
        functools.partial(expert_weight_kernel, 2 * flat // block),
        grid=(3 * flat // block,),
        in_specs=[full, full, pl.BlockSpec((seq, block), lambda j: (0, j))],
        out_specs=pl.BlockSpec((width, block), lambda j: (0, j)),
        out_shape=jax.ShapeDtypeStruct((width, 3 * flat), BF),
        compiler_params=params(56),
    )(in_hbm(normed), cot, acts)


def product_kernel(count, form, turn_ref, *refs):
    total = form(refs[0][...], refs[count][...])
    for i in range(1, count):
        total = total + form(refs[i][...], refs[count + i][...])
    refs[2 * count][...] = total.astype(refs[2 * count].dtype)


def product(form, lefts, rights, rows, steps, block, kind, turn):
    return pl.pallas_call(
        functools.partial(product_kernel, len(lefts), form),
        grid_spec=pltpu.PrefetchScalarGridSpec(
            num_scalar_prefetch=1,
            grid=(steps,),
            in_specs=[pl.BlockSpec(shape, index) for _, shape, index in lefts + rights],
            out_specs=pl.BlockSpec((rows, block), lambda i, turn_ref: (0, i)),
        ),
        out_shape=jax.ShapeDtypeStruct((rows, steps * block), kind),
        compiler_params=params(56),
    )(turn.reshape(1), *[item[0] for item in lefts + rights])


def fold(keep, received):
    return (keep.astype(F32) + received.astype(F32)).astype(BF)


def sum_all(value):
    for bit in range(bits_of(lax.axis_size("dp"))):
        value = value + swap(value, bit)
    return value + swap_pair(value)


class Reduction:
    def __init__(self, lefts, right, order, ready, *needed):
        self.order = list(order)
        self.lefts, self.right = lefts, right
        self.rows = 2 * lefts[0].shape[1] // lax.axis_size("dp")
        self.axes = list(range(1, bits_of(lax.axis_size("dp"))))
        self.sent = dot_tn(after(lefts[1], *needed), right).astype(BF)
        self.got = swap(tie(self.sent, *ready), 0)

    def total(self, *needed):
        total = dot_tn(after(self.lefts[0], *needed), self.right) + self.got.astype(F32)
        return total.astype(BF).reshape((2,) * len(self.axes) + (self.rows, -1))

    def keep(self, *needed):
        held = self.total(*needed)
        self.send(held)
        return held

    def keep_two(self, other, cut, *needed):
        held = self.total(*needed)
        rest = Reduction.__new__(Reduction)
        rest.order, rest.axes = list(other), list(self.axes)
        self.send(held[..., :cut])
        rest.send(held[..., cut:])
        return rest, held

    def send(self, held):
        axis = self.axes.index(self.order[0])
        self.mine = lax.index_in_dim(held, 0, axis, keepdims=False)
        self.got = swap(lax.index_in_dim(held, 1, axis, keepdims=False), self.order[0])

    def fold(self, *needed):
        self.axes.remove(self.order.pop(0))
        mine = after(self.mine, *needed) if needed else self.mine
        return fold(mine, self.got)

    def step(self, *needed):
        held = self.fold(*needed)
        self.send(held)
        return held

    def join(self, other, *needed):
        held = jnp.concatenate([self.fold(*needed), other.fold(*needed)], axis=-1)
        self.send(held)
        return held

    def finish(self, *needed):
        while len(self.order) > 1:
            self.step(*needed)
        self.axes.remove(self.order.pop(0))
        return after(self.mine, *needed).astype(F32) + self.got.astype(F32)


def body(
    tokens, cotangent, routes, route_weights, query_weight, key_weight, value_weight, out_weight,
    gate_weight, up_weight, down_weight, attn_gain, ffn_gain, query_gain, key_gain,
):
    turn = lax.axis_index("tensor").astype(jnp.int32)
    chunk = tokens.shape[0]
    seq = 2 * chunk
    width = tokens.shape[1]
    order = block_order()
    plain = lax.iota(jnp.int32, order.shape[0])
    cosine, sine = rope_tables(seq)
    experts, hidden_cols = gate_weight.shape[2], gate_weight.shape[3]
    flat = experts * hidden_cols
    q_cols, kv_cols = query_weight.shape[2], key_weight.shape[2]
    bits = bits_of(lax.axis_size("dp"))
    straight = list(range(1, bits))
    crossed = straight if bits < 3 else [2, 1] + straight[2:]
    wide, tall = min(512, 2 * kv_cols), min(512, width)

    def select(zero, one):
        return jnp.where(turn == 0, zero, one)

    attn_w = lax.all_gather(
        jnp.concatenate([out_weight[0], query_weight[0], key_weight[0], value_weight[0]], axis=1),
        "dp", axis=0, tiled=True,
    )
    ffn_w = lax.all_gather(
        jnp.concatenate([w[0].reshape(-1, flat) for w in (gate_weight, up_weight, down_weight)], axis=1),
        "dp", axis=0, tiled=True,
    )

    tokens_other = swap_pair(tokens)
    cot_other = swap_pair(after(cotangent, tokens_other))
    (tokens_all,) = join(tokens, tokens_other, turn, plain, 1)
    resid = tokens_all.astype(F32)
    normed = (resid * mean_square(resid) * attn_gain).astype(BF)
    normed_rel = join(normed[:chunk], normed[chunk:], 0, order, 2)

    raw = product(
        dot,
        [(after(normed, normed_rel), (seq, width), lambda i, t: (0, 0))],
        [(attn_w, (width, wide), lambda i, t: (0, q_cols // wide + i))],
        seq, (q_cols + 2 * kv_cols) // wide, wide, F32, turn,
    )
    lse, part, got = {}, {}, {}
    context = None
    for index in (1, 0):
        context, lse[index] = attention_fwd(
            raw, q_cols, kv_cols, chunk, index, query_gain, key_gain, cosine, sine, context
        )
        part[index] = product(
            dot_nt,
            [(in_hbm(context), (chunk, q_cols), lambda i, t, index=index: (index, 0))],
            [(attn_w, (tall, q_cols), lambda i, t: (i, 0))],
            chunk, width // tall, tall, BF, turn,
        )
        got[index] = swap_pair(part[index])
        last = part[index]
        context = after(context, last)

    cot_other = after(cot_other, last)
    (cot_all,) = join(cotangent, cot_other, turn, plain, 1)
    last = cot_all

    mid, back_part, back_got = {}, {}, {}
    normed_f = None
    acts = None
    for index in (1, 0):
        mid[index], normed_f = middle(tokens_all, after(part[index], last), got[index], ffn_gain, index, normed_f)
        acts = expert_part(normed_f, cot_all, ffn_w, routes[0], route_weights[0], index, experts, acts)
        if index == 0:
            ffn_parts_grad = expert_weights(normed_f, cot_all, acts, wide)
            ffn_grad = lax.psum_scatter(ffn_parts_grad, "dp", scatter_dimension=0, tiled=True).astype(F32)
            acts = after(acts, ffn_parts_grad)
        back_part[index] = product(
            dot_nt,
            [(acts, (chunk, 2 * flat), lambda i, t, index=index: (index, 0))],
            [(ffn_w, (tall, 2 * flat), lambda i, t: (i, 0))],
            chunk, width // tall, tall, BF, turn,
        )
        if index == 0:
            back_part[0] = tie(back_part[0], back_got[1])
        back_got[index] = swap_pair(back_part[index])
        last = back_part[index]
        acts, normed_f = after(acts, last), after(normed_f, last)

    def expert_out(who, *needed):
        return product(
            dot_nt,
            [(after(acts, *needed), (chunk, flat), lambda i, t: (who(t[0]), 2))],
            [(ffn_w, (tall, flat), lambda i, t: (i, 2))],
            chunk, width // tall, tall, BF, turn,
        )

    grad_mid, grad_mid_b, ffn_parts, grad_context = {}, {}, {}, {}
    earlier = None
    for index in (1, 0):
        grad_mid[index], grad_mid_b[index], ffn_parts[index] = middle_back(
            cot_all, after(back_part[index], last), back_got[index], mid[index], ffn_gain, index
        )
        grad_context[index] = product(
            dot,
            [(grad_mid_b[index], (chunk, width), lambda i, t: (0, 0))],
            [(attn_w, (width, wide), lambda i, t: (0, i))],
            chunk, q_cols // wide, wide, BF, turn,
        )
        last = grad_context[index]
        if index == 0:
            grad_mid_rel = join(after(grad_mid_b[0], last), grad_mid_b[1], 0, order, 2)
            out_sum = Reduction(grad_mid_rel, context, straight, [])
            out_theirs = expert_out(lambda t: 1 - t, out_sum.sent)
            out_got = swap_pair(tie(out_theirs, back_got[0]))
            last = out_sum.keep(out_theirs)
        dq, dk, dv, query_part, key_part = attention_bwd(
            raw, q_cols, kv_cols, chunk, index, context, after(grad_context[index], last), lse[index],
            query_gain, key_gain, cosine, sine, earlier, index == 0,
        )
        earlier = (dk, dv, query_part, dq)
        last = dq

    dkv = jnp.concatenate([dk, dv], axis=1)

    def normed_back(who, *needed):
        return product(
            dot_nt,
            [
                (after(dq, *needed), (chunk, q_cols), lambda i, t: (who(t[0]), 0)),
                (dkv, (chunk, 2 * kv_cols), lambda i, t: (who(t[0]), 0)),
            ],
            [
                (attn_w, (tall, q_cols), lambda i, t: (i, 1)),
                (attn_w, (tall, 2 * kv_cols), lambda i, t: (i, q_cols // kv_cols)),
            ],
            chunk, width // tall, tall, BF, turn,
        )

    grad_qkv = jnp.concatenate([dq, dkv], axis=1)
    qkv_sum = Reduction(normed_rel, grad_qkv, straight, [])
    grad_theirs = normed_back(lambda t: 1 - t, qkv_sum.sent)
    rest_sum, last = qkv_sum.keep_two(crossed, grad_qkv.shape[1] // 2, grad_theirs)
    grad_got = swap_pair(grad_theirs)
    last = out_sum.step(last)
    grad_mine = normed_back(lambda t: t, last)
    out_mine = expert_out(lambda t: t, grad_mine)
    last = qkv_sum.step(out_mine)
    last = rest_sum.step(last)
    last = out_sum.step(last)
    output = (select(mid[0], mid[1]) + (after(out_mine, last).astype(F32) + out_got.astype(F32))).astype(BF)
    last = qkv_sum.step(output)
    last = rest_sum.step(last)
    grad_normed = after(grad_mine, last).astype(F32) + grad_got.astype(F32)
    grad_one, attn_part = norm_back(tokens.astype(F32), attn_gain, grad_normed)
    tokens_grad = select(grad_mid[0], grad_mid[1]) + grad_one
    ffn_part = (ffn_parts[0] + ffn_parts[1]) * 0.5
    small = jnp.concatenate([attn_part, ffn_part, query_part, key_part], axis=1)
    small = sum_all(small)
    out_grad = out_sum.finish(tokens_grad)
    rest_grad = rest_sum.finish(out_grad)
    qkv_grad = jnp.concatenate([qkv_sum.finish(rest_grad), rest_grad], axis=1)

    def expert(index):
        return ffn_grad[:, index * flat : (index + 1) * flat].reshape(1, -1, experts, hidden_cols)

    return (
        output,
        tokens_grad,
        qkv_grad[None, :, :q_cols],
        qkv_grad[None, :, q_cols : q_cols + kv_cols],
        qkv_grad[None, :, q_cols + kv_cols :],
        out_grad[None],
        expert(0),
        expert(1),
        expert(2),
        small[:, :width],
        small[:, width : 2 * width],
        small[:, 2 * width : 2 * width + HD],
        small[:, 2 * width + HD :],
    )


def solution(mesh):
    return jax.shard_map(
        body,
        mesh=mesh,
        in_specs=(
            P(("dp", "tensor"), None),
            P(("dp", "tensor"), None),
            P(None, "dp", None),
            P(None, "dp", None),
            P(None, "dp", "tensor"),
            P(None, "dp", "tensor"),
            P(None, "dp", "tensor"),
            P(None, "dp", "tensor"),
            P(None, "dp", None, "tensor"),
            P(None, "dp", None, "tensor"),
            P(None, "dp", None, "tensor"),
            P(),
            P(),
            P(),
            P(),
        ),
        out_specs=(
            P(("dp", "tensor"), None),
            P(("dp", "tensor"), None),
            P(None, "dp", "tensor"),
            P(None, "dp", "tensor"),
            P(None, "dp", "tensor"),
            P(None, "dp", "tensor"),
            P(None, "dp", None, "tensor"),
            P(None, "dp", None, "tensor"),
            P(None, "dp", None, "tensor"),
            P(),
            P(),
            P(),
            P(),
        ),
        check_vma=False,
    )
```

```python
import functools
import math

import jax
import jax.numpy as jnp
import numpy as np
from jax import lax
from jax.experimental import pallas as pl
from jax.experimental.pallas import tpu as pltpu
from jax.sharding import PartitionSpec as P

HD = 128
EPS = 1e-06
THETA = 1000000.0
SCALE = HD ** -0.5
LOG2E = math.log2(math.e)
NT = (((1,), (1,)), ((), ()))
BF = jnp.bfloat16
F32 = jnp.float32


def params(mib):
    return pltpu.CompilerParams(vmem_limit_bytes=mib * 2**20)


def dot(left, right):
    return jnp.dot(left, right, preferred_element_type=F32)


def dot_nt(left, right):
    return lax.dot_general(left, right, NT, preferred_element_type=F32)


def dot_tn(left, right):
    return lax.dot_general(left, right, (((0,), (0,)), ((), ())), preferred_element_type=F32)


def head_norm(values, gain, cosine, sine):
    scale = lax.rsqrt(jnp.mean(values * values, axis=-1, keepdims=True) + EPS)
    normed = values * scale * gain
    return normed * cosine + pltpu.roll(normed, HD // 2, 1) * sine


def head_norm_back(values, gain, cosine, sine, grad_rot):
    scale = lax.rsqrt(jnp.mean(values * values, axis=-1, keepdims=True) + EPS)
    grad = grad_rot * cosine - pltpu.roll(grad_rot, HD // 2, 1) * sine
    scaled = grad * gain
    inner = jnp.mean(scaled * values, axis=-1, keepdims=True)
    grad_values = scale * scaled - values * (scale * scale * scale) * inner
    return grad_values, jnp.sum(grad * values * scale, axis=0, keepdims=True)


def causal(offset, rows, columns):
    key = lax.broadcasted_iota(jnp.int32, (rows, columns), 0) + offset
    return key <= lax.broadcasted_iota(jnp.int32, (rows, columns), 1)


def attn_fwd_kernel(block, q_ref, k_ref, v_ref, qg_ref, kg_ref, qcos_ref, qsin_ref, kcos_ref, ksin_ref, *rest):
    out_ref, lse_ref, qs, ks, vt, ps, ss, mix, sums = rest[-9:]
    chunk, per = q_ref.shape[0], q_ref.shape[1] // HD
    base = k_ref.shape[0] - chunk
    tile = min(64, block)

    @pl.when(pl.program_id(1) == 0)
    def _():
        ks[...] = head_norm(k_ref[...], kg_ref[...], kcos_ref[...], ksin_ref[...]).astype(BF)
        vt[...] = v_ref[...].astype(BF).T

    for h in range(per):
        lanes = slice(h * HD, (h + 1) * HD)
        qs[h] = head_norm(q_ref[:, lanes], qg_ref[...], qcos_ref[...], qsin_ref[...]).astype(BF)
    pairs = [(h, i) for h in range(per) for i in range(chunk // block)]

    def place(h, i):
        start = base + i * block
        return slice(h * HD, (h + 1) * HD), slice(i * block, (i + 1) * block), start, start + block

    for h, i in pairs:
        lanes, cols, start, end = place(h, i)
        ss[h, :end, cols] = dot_nt(ks[:end], qs[h, cols])
    for h, i in pairs:
        lanes, cols, start, end = place(h, i)
        total = jnp.zeros((8, block), F32)
        for r in range(0, end, tile):
            probs = jnp.exp2(ss[h, r : r + tile, cols] * (SCALE * LOG2E))
            if r >= start:
                probs = jnp.where(causal(r - start, tile, block), probs, 0.0)
            total = total + jnp.sum(probs.reshape(tile // 8, 8, block), axis=0)
            ps[h, r : r + tile, cols] = probs.astype(BF)
        sums[h, :, cols] = jnp.sum(total, axis=0, keepdims=True)
    for h, i in pairs:
        lanes, cols, start, end = place(h, i)
        mix[h, :, cols] = dot(vt[:, :end], ps[h, :end, cols])
    for h, i in pairs:
        lanes, cols, start, end = place(h, i)
        out_ref[cols, lanes] = (mix[h, :, cols] * (1.0 / sums[h, :, cols])).T.astype(BF)
    lse_ref[...] = jnp.log2(sums[...])


def attn_specs(raw, q_cols, kv_cols, chunk, index, per):
    heads, kv = q_cols // HD, kv_cols // HD
    steps = heads // kv // per
    keys = (index + 1) * chunk
    head_in = pl.BlockSpec((chunk, per * HD), lambda k, g: (index, k * steps + g))
    head = pl.BlockSpec((chunk, per * HD), lambda k, g: (0, k * steps + g))
    lse = pl.BlockSpec((per, 1, chunk), lambda k, g: (k * steps + g, 0, 0))
    gain = pl.BlockSpec((1, HD), lambda k, g: (0, 0))
    query_table = pl.BlockSpec((chunk, HD), lambda k, g: (index, 0))

    def of_keys(rows):
        return (
            pl.BlockSpec((rows, HD), lambda k, g: (0, heads + k)),
            pl.BlockSpec((rows, HD), lambda k, g: (0, heads + kv + k)),
            pl.BlockSpec((rows, HD), lambda k, g: (0, 0)),
            pl.BlockSpec((rows, HD), lambda k, g: (0, k)),
        )

    return heads, kv, steps, keys, head_in, head, lse, gain, query_table, of_keys


def attention_fwd(raw, q_cols, kv_cols, chunk, index, query_g, key_g, cosine, sine, earlier):
    seq = raw.shape[0]
    more = [] if earlier is None else [earlier]
    per = min(4, q_cols // kv_cols)
    heads, kv, steps, keys, head_in, head, lse, gain, query_table, of_keys = attn_specs(
        raw, q_cols, kv_cols, chunk, index, per
    )
    key_in, value_in, key_table, _ = of_keys(keys)
    return pl.pallas_call(
        functools.partial(attn_fwd_kernel, min(256, chunk)),
        grid=(kv, steps),
        in_specs=[head_in, key_in, value_in, gain, gain, query_table, query_table, key_table, key_table]
        + [pl.BlockSpec(memory_space=pl.ANY)] * len(more),
        out_specs=[head_in, lse],
        out_shape=[
            pltpu.HBM((seq, heads * HD), BF),
            jax.ShapeDtypeStruct((heads, 1, chunk), F32),
        ],
        scratch_shapes=[
            pltpu.VMEM((per, chunk, HD), BF),
            pltpu.VMEM((keys, HD), BF),
            pltpu.VMEM((HD, keys), BF),
            pltpu.VMEM((per, keys, chunk), BF),
            pltpu.VMEM((per, keys, chunk), F32),
            pltpu.VMEM((per, HD, chunk), F32),
            pltpu.VMEM((per, 1, chunk), F32),
        ],
        input_output_aliases={9: 0} if more else {},
        compiler_params=params(48),
    )(raw, raw, raw, query_g, key_g, cosine, sine, cosine, sine, *more)


def attn_bwd_kernel(
    block, keys, first, last, q_ref, k_ref, v_ref, ctx_ref, grad_ref, lse_ref, qg_ref, kg_ref,
    qcos_ref, qsin_ref, kcos_ref, ksin_ref, *rest,
):
    if first:
        dq_ref, dk_ref, dv_ref, dqg_ref, dkg_ref, qs, ks, kt, vs, ps, ds, dks, dvs, ss, gs, deltas, dqs = rest
    else:
        (dk_in, dv_in, dqg_in, dq_in, dq_ref, dk_ref, dv_ref, dqg_ref, dkg_ref,
         qs, ks, kt, vs, ps, ds, dks, dvs, ss, gs, deltas, dqs) = rest
    chunk, per = q_ref.shape[0], q_ref.shape[1] // HD
    base = (keys - chunk) // block
    kv_id, g_id = pl.program_id(0), pl.program_id(1)

    @pl.when(g_id == 0)
    def _():
        rotated = head_norm(k_ref[:keys], kg_ref[...], kcos_ref[:keys], ksin_ref[:keys]).astype(BF)
        ks[...] = rotated
        kt[...] = rotated.T
        vs[...] = v_ref[:keys].astype(BF)
        dks[...] = jnp.zeros_like(dks) if first else dk_in[...]
        dvs[...] = jnp.zeros_like(dvs) if first else dv_in[...]

    @pl.when((g_id == 0) & (kv_id == 0))
    def _():
        dqg_ref[...] = jnp.zeros_like(dqg_ref) if first else dqg_in[...]
        dkg_ref[...] = jnp.zeros_like(dkg_ref)

    tile = min(64, block)
    for h in range(per):
        lanes = slice(h * HD, (h + 1) * HD)
        qs[h] = head_norm(q_ref[:, lanes], qg_ref[...], qcos_ref[...], qsin_ref[...]).astype(BF)
    pairs = [(h, i) for h in range(per) for i in range(chunk // block)]

    def place(h, i):
        start = (base + i) * block
        return slice(h * HD, (h + 1) * HD), slice(i * block, (i + 1) * block), start, start + block

    def first_products(h):
        for i in range(chunk // block):
            lanes, cols, start, end = place(h, i)
            product = grad_ref[cols, lanes].astype(F32) * ctx_ref[cols, lanes].astype(F32)
            deltas[h, :, cols] = jnp.sum(product.T, axis=0, keepdims=True)
            ss[h % 2, :end, cols] = dot_nt(ks[:end], qs[h, cols])
            gs[h % 2, :end, cols] = dot_nt(vs[:end], grad_ref[cols, lanes])

    def weights(h):
        for i in range(chunk // block):
            lanes, cols, start, end = place(h, i)
            delta, lse = deltas[h, :, cols], lse_ref[h, :, cols]
            for r in range(0, end, tile):
                rows = slice(r, r + tile)
                probs = jnp.exp2(ss[h % 2, rows, cols] * (SCALE * LOG2E) - lse)
                if r >= start:
                    probs = jnp.where(causal(r - start, tile, block), probs, 0.0)
                ps[h % 2, rows, cols] = probs.astype(BF)
                ds[h % 2, rows, cols] = (probs * (gs[h % 2, rows, cols] - delta)).astype(BF)

    def second_products(h):
        lanes = slice(h * HD, (h + 1) * HD)
        for j in range(keys // block):
            rows = slice(j * block, (j + 1) * block)
            start = max(0, j - base) * block
            dvs[rows] += dot(ps[h % 2, rows, start:], grad_ref[start:, lanes])
            dks[rows] += dot(ds[h % 2, rows, start:], qs[h, start:])
        for i in range(chunk // block):
            lanes, cols, start, end = place(h, i)
            dqs[h % 2, :, cols] = dot(kt[:, :end], ds[h % 2, :end, cols])

    def last_part(h):
        total = jnp.zeros((1, HD), F32)
        for i in range(chunk // block):
            lanes, cols, start, end = place(h, i)
            grad_raw, part = head_norm_back(
                q_ref[cols, lanes], qg_ref[...], qcos_ref[cols], qsin_ref[cols], dqs[h % 2, :, cols].T * SCALE
            )
            dq_ref[cols, lanes] = grad_raw.astype(BF)
            total = total + part
        return total

    gain_sum = jnp.zeros((1, HD), F32)
    first_products(0)
    for h in range(per):
        if h + 1 < per:
            first_products(h + 1)
        weights(h)
        if h:
            gain_sum = gain_sum + last_part(h - 1)
        second_products(h)
    gain_sum = gain_sum + last_part(per - 1)
    dqg_ref[...] += gain_sum

    @pl.when(g_id == pl.num_programs(1) - 1)
    def _():
        if last:
            grad_raw, part = head_norm_back(k_ref[...], kg_ref[...], kcos_ref[...], ksin_ref[...], dks[...] * SCALE)
            dk_ref[...] = grad_raw.astype(BF)
            dv_ref[...] = dvs[...].astype(BF)
            dkg_ref[...] += part
        else:
            dk_ref[...] = dks[...]
            dv_ref[...] = dvs[...]


def attention_bwd(
    raw, q_cols, kv_cols, chunk, index, context, grad_context, lse_rows, query_g, key_g, cosine, sine, earlier, last
):
    seq = raw.shape[0]
    per = min(4, q_cols // kv_cols)
    heads, kv, steps, keys, head_in, head, lse, gain, query_table, of_keys = attn_specs(
        raw, q_cols, kv_cols, chunk, index, per
    )
    key_in, value_in, key_table, key_out = of_keys(seq)
    first = earlier is None
    more = [] if first else list(earlier)
    kind = BF if last else F32
    return pl.pallas_call(
        functools.partial(attn_bwd_kernel, min(256, chunk), keys, first, last),
        grid=(kv, steps),
        in_specs=[head_in, key_in, value_in, head_in, head, lse, gain, gain, query_table, query_table, key_table, key_table]
        + ([] if first else [key_out, key_out, gain, pl.BlockSpec(memory_space=pl.ANY)]),
        out_specs=[head_in, key_out, key_out, gain, gain],
        out_shape=[
            jax.ShapeDtypeStruct((seq, heads * HD), BF),
            jax.ShapeDtypeStruct((seq, kv * HD), kind),
            jax.ShapeDtypeStruct((seq, kv * HD), kind),
            jax.ShapeDtypeStruct((1, HD), F32),
            jax.ShapeDtypeStruct((1, HD), F32),
        ],
        scratch_shapes=[
            pltpu.VMEM((per, chunk, HD), BF),
            pltpu.VMEM((keys, HD), BF),
            pltpu.VMEM((HD, keys), BF),
            pltpu.VMEM((keys, HD), BF),
            pltpu.VMEM((2, keys, chunk), BF),
            pltpu.VMEM((2, keys, chunk), BF),
            pltpu.VMEM((seq, HD), F32),
            pltpu.VMEM((seq, HD), F32),
            pltpu.VMEM((2, keys, chunk), F32),
            pltpu.VMEM((2, keys, chunk), F32),
            pltpu.VMEM((per, 1, chunk), F32),
            pltpu.VMEM((2, HD, chunk), F32),
        ],
        input_output_aliases={} if first else {15: 0},
        compiler_params=params(58),
    )(raw, raw, raw, in_hbm(context), grad_context, lse_rows, query_g, key_g, cosine, sine, cosine, sine, *more)


def rope_tables(seq):
    position = lax.iota(F32, seq)
    freq = THETA ** (-2.0 * lax.iota(F32, HD // 2) / HD)
    angle = position[:, None] * freq[None, :]
    cosine, sine = jnp.cos(angle), jnp.sin(angle)
    return jnp.concatenate([cosine, cosine], axis=1), jnp.concatenate([-sine, sine], axis=1)


def bits_of(count):
    return count.bit_length() - 1


def swap(value, bit):
    count = lax.axis_size("dp")
    return lax.ppermute(value, "dp", [(i, i ^ (1 << bit)) for i in range(count)])


def swap_pair(value):
    return lax.ppermute(value, "tensor", [(0, 1), (1, 0)])


def after(value, *needed):
    return lax.optimization_barrier((value, needed))[0]


def in_hbm(value):
    return pltpu.with_memory_space_constraint(value, pltpu.HBM)


def tie_kernel(*refs):
    pass


def tie(value, *needed):
    anywhere = pl.BlockSpec(memory_space=pl.ANY)
    return pl.pallas_call(
        tie_kernel,
        in_specs=[anywhere] * (1 + len(needed)),
        out_specs=anywhere,
        out_shape=jax.ShapeDtypeStruct(value.shape, value.dtype),
        input_output_aliases={0: 0},
    )(value, *needed)


def block_order():
    count = lax.axis_size("dp")
    bits = bits_of(count)
    reverse = np.array([int(format(i, "b").zfill(bits)[::-1], 2) if bits else 0 for i in range(count)], np.int32)
    return jnp.asarray(reverse) ^ lax.axis_index("dp").astype(jnp.int32)


def join_kernel(count, parts, turn_ref, order_ref, one_ref, two_ref, *out_refs):
    block = one_ref.shape[1] // count

    def fill(ref):
        for i in range(count):
            column = pl.multiple_of(order_ref[i] * block, block)
            out_ref, at = out_refs[i // (count // parts)], i % (count // parts)
            out_ref[:, at * block : (at + 1) * block] = ref[:, pl.ds(column, block)]

    @pl.when(pl.program_id(0) == turn_ref[0])
    def _():
        fill(one_ref)

    @pl.when(pl.program_id(0) != turn_ref[0])
    def _():
        fill(two_ref)


def join(one, two, turn, order, parts):
    rows, width = one.shape
    count = order.shape[0]
    tile = min(256, rows)
    turn = jnp.asarray(turn, jnp.int32)
    if (width // count) % 128:
        both = jnp.where(turn == 0, jnp.concatenate([one, two], axis=0), jnp.concatenate([two, one], axis=0))
        both = jnp.take(both.reshape(2 * rows, count, -1), order, axis=1).reshape(2 * rows, width)
        return jnp.split(both, parts, axis=1)
    steps = rows // tile
    half = pl.BlockSpec((tile, width), lambda h, r: (r, 0))
    scalar = pl.BlockSpec(memory_space=pltpu.SMEM)
    return pl.pallas_call(
        functools.partial(join_kernel, count, parts),
        grid=(2, steps),
        in_specs=[scalar, scalar, half, half],
        out_specs=[pl.BlockSpec((tile, width // parts), lambda h, r: (h * steps + r, 0))] * parts,
        out_shape=[jax.ShapeDtypeStruct((2 * rows, width // parts), one.dtype)] * parts,
        compiler_params=params(32),
    )(turn.reshape(1), order, one, two)


def mean_square(values):
    return lax.rsqrt(jnp.mean(values * values, axis=-1, keepdims=True) + EPS)


def mid_kernel(base_ref, part_ref, got_ref, gain_ref, *rest):
    mid_ref, normed_ref = rest[-2:]
    mid = base_ref[...].astype(F32) + (part_ref[...].astype(F32) + got_ref[...].astype(F32))
    mid_ref[...] = mid
    normed_ref[...] = (mid * mean_square(mid) * gain_ref[...]).astype(BF)


def middle(base, part, got, gain, index, earlier):
    rows, width = part.shape
    tile = min(128, rows)
    block = pl.BlockSpec((tile, width), lambda r: (r, 0))
    place = pl.BlockSpec((tile, width), lambda r: (index * (rows // tile) + r, 0))
    more = [] if earlier is None else [earlier]
    return pl.pallas_call(
        mid_kernel,
        grid=(rows // tile,),
        in_specs=[place, block, block, pl.BlockSpec((1, width), lambda r: (0, 0))]
        + [pl.BlockSpec(memory_space=pl.ANY)] * len(more),
        out_specs=[block, place],
        out_shape=[pltpu.HBM((rows, width), F32), pltpu.HBM(base.shape, BF)],
        input_output_aliases={4: 1} if more else {},
        compiler_params=params(32),
    )(base, part, got, gain, *more)


def norm_back(values, gain, grad):
    scale = mean_square(values)
    scaled = grad * gain
    inner = jnp.mean(scaled * values, axis=-1, keepdims=True)
    grad_values = scale * scaled - values * (scale * scale * scale) * inner
    return grad_values, jnp.sum(grad * values * scale, axis=0, keepdims=True)


def mid_back_kernel(base_ref, part_ref, got_ref, mid_ref, gain_ref, out_ref, low_ref, sum_ref):
    grad = part_ref[...].astype(F32) + got_ref[...].astype(F32)
    back, part = norm_back(mid_ref[...], gain_ref[...], grad)
    total = base_ref[...].astype(F32) + back
    out_ref[...] = total
    low_ref[...] = total.astype(BF)

    @pl.when(pl.program_id(0) == 0)
    def _():
        sum_ref[...] = jnp.zeros_like(sum_ref)

    sum_ref[...] += part


def middle_back(base, part, got, mid, gain, index):
    rows, width = part.shape
    tile = min(128, rows)
    block = pl.BlockSpec((tile, width), lambda r: (r, 0))
    line = pl.BlockSpec((1, width), lambda r: (0, 0))
    return pl.pallas_call(
        mid_back_kernel,
        grid=(rows // tile,),
        in_specs=[pl.BlockSpec((tile, width), lambda r: (index * (rows // tile) + r, 0)), block, block, block, line],
        out_specs=[block, block, line],
        out_shape=[
            pltpu.HBM((rows, width), F32),
            jax.ShapeDtypeStruct((rows, width), BF),
            jax.ShapeDtypeStruct((1, width), F32),
        ],
        compiler_params=params(32),
    )(base, part, got, in_hbm(mid), gain)


def expert_kernel(unit, cols, x_ref, cot_ref, gate_ref, up_ref, down_ref, route_ref, weight_ref, *rest):
    out_ref = rest[-1]
    step, count = pl.program_id(0), pl.num_programs(0)
    rows, block = x_ref.shape[0], gate_ref.shape[1]
    tile = min(256, rows)

    def place(kind):
        return pl.ds(pl.multiple_of((kind * count + step) * block, block), block)

    for r in range(rows // tile):
        part = slice(r * tile, (r + 1) * tile)
        shares = []
        for k in range(block // unit):
            expert = (step * (block // unit) + k) // (cols // unit)
            share = jnp.sum(jnp.where(route_ref[part] == expert, weight_ref[part], 0.0), axis=-1, keepdims=True)
            shares.append(jnp.broadcast_to(share, (tile, unit)))
        share = jnp.concatenate(shares, axis=1)
        gate = dot(x_ref[part], gate_ref[...])
        up = dot(x_ref[part], up_ref[...])
        grad_hidden = dot(cot_ref[part], down_ref[...]) * share
        sigma = 1.0 / (1.0 + jnp.exp(-gate))
        silu = gate * sigma
        out_ref[part, place(0)] = (grad_hidden * up * (sigma + silu * (1.0 - sigma))).astype(BF)
        out_ref[part, place(1)] = (grad_hidden * silu).astype(BF)
        out_ref[part, place(2)] = (silu * up * share).astype(BF)


def expert_part(normed, cot, weights, routes, route_weights, index, experts, earlier):
    width = normed.shape[1]
    flat = weights.shape[1] // 3
    cols = flat // experts
    unit = math.gcd(cols, 128)
    block = 2 * unit if flat % (2 * unit) == 0 else unit
    steps = flat // block
    seq = routes.shape[0]
    rows = seq // 2
    pair = pl.BlockSpec((rows, routes.shape[1]), lambda e: (index, 0))
    half = pl.BlockSpec((rows, width), lambda e: (index, 0))
    more = [] if earlier is None else [earlier]
    return pl.pallas_call(
        functools.partial(expert_kernel, unit, cols),
        grid=(steps,),
        in_specs=[half, half]
        + [pl.BlockSpec((width, block), lambda e, k=k: (0, k * steps + e)) for k in range(3)]
        + [pair, pair]
        + [pl.BlockSpec(memory_space=pl.ANY)] * len(more),
        out_specs=pl.BlockSpec((rows, 3 * flat), lambda e: (index, 0)),
        out_shape=jax.ShapeDtypeStruct((seq, 3 * flat), BF),
        input_output_aliases={7: 0} if more else {},
        compiler_params=params(56),
    )(in_hbm(normed), cot, weights, weights, weights, routes, route_weights, *more)


def expert_weight_kernel(cut, normed_ref, cot_ref, act_ref, out_ref):
    step = pl.program_id(0)

    @pl.when(step < cut)
    def _():
        out_ref[...] = dot_tn(normed_ref[...], act_ref[...]).astype(BF)

    @pl.when(step >= cut)
    def _():
        out_ref[...] = dot_tn(cot_ref[...], act_ref[...]).astype(BF)


def expert_weights(normed, cot, acts, block):
    seq, width = normed.shape
    flat = acts.shape[1] // 3
    full = pl.BlockSpec((seq, width), lambda j: (0, 0))
    return pl.pallas_call(
        functools.partial(expert_weight_kernel, 2 * flat // block),
        grid=(3 * flat // block,),
        in_specs=[full, full, pl.BlockSpec((seq, block), lambda j: (0, j))],
        out_specs=pl.BlockSpec((width, block), lambda j: (0, j)),
        out_shape=jax.ShapeDtypeStruct((width, 3 * flat), BF),
        compiler_params=params(56),
    )(in_hbm(normed), cot, acts)


def product_kernel(count, form, turn_ref, *refs):
    total = form(refs[0][...], refs[count][...])
    for i in range(1, count):
        total = total + form(refs[i][...], refs[count + i][...])
    refs[2 * count][...] = total.astype(refs[2 * count].dtype)


def product(form, lefts, rights, rows, steps, block, kind, turn):
    return pl.pallas_call(
        functools.partial(product_kernel, len(lefts), form),
        grid_spec=pltpu.PrefetchScalarGridSpec(
            num_scalar_prefetch=1,
            grid=(steps,),
            in_specs=[pl.BlockSpec(shape, index) for _, shape, index in lefts + rights],
            out_specs=pl.BlockSpec((rows, block), lambda i, turn_ref: (0, i)),
        ),
        out_shape=jax.ShapeDtypeStruct((rows, steps * block), kind),
        compiler_params=params(56),
    )(turn.reshape(1), *[item[0] for item in lefts + rights])


def fold(keep, received):
    return (keep.astype(F32) + received.astype(F32)).astype(BF)


def sum_all(value):
    for bit in range(bits_of(lax.axis_size("dp"))):
        value = value + swap(value, bit)
    return value + swap_pair(value)


class Reduction:
    def __init__(self, lefts, right, order, ready, *needed):
        self.order = list(order)
        self.lefts, self.right = lefts, right
        self.rows = 2 * lefts[0].shape[1] // lax.axis_size("dp")
        self.axes = list(range(1, bits_of(lax.axis_size("dp"))))
        self.sent = dot_tn(after(lefts[1], *needed), right).astype(BF)
        self.got = swap(tie(self.sent, *ready), 0)

    def total(self, *needed):
        total = dot_tn(after(self.lefts[0], *needed), self.right) + self.got.astype(F32)
        return total.astype(BF).reshape((2,) * len(self.axes) + (self.rows, -1))

    def keep(self, *needed):
        held = self.total(*needed)
        self.send(held)
        return held

    def keep_two(self, other, cut, *needed):
        held = self.total(*needed)
        rest = Reduction.__new__(Reduction)
        rest.order, rest.axes = list(other), list(self.axes)
        self.send(held[..., :cut])
        rest.send(held[..., cut:])
        return rest, held

    def send(self, held):
        axis = self.axes.index(self.order[0])
        self.mine = lax.index_in_dim(held, 0, axis, keepdims=False)
        self.got = swap(lax.index_in_dim(held, 1, axis, keepdims=False), self.order[0])

    def fold(self, *needed):
        self.axes.remove(self.order.pop(0))
        mine = after(self.mine, *needed) if needed else self.mine
        return fold(mine, self.got)

    def step(self, *needed):
        held = self.fold(*needed)
        self.send(held)
        return held

    def join(self, other, *needed):
        held = jnp.concatenate([self.fold(*needed), other.fold(*needed)], axis=-1)
        self.send(held)
        return held

    def finish(self, *needed):
        while len(self.order) > 1:
            self.step(*needed)
        self.axes.remove(self.order.pop(0))
        return after(self.mine, *needed).astype(F32) + self.got.astype(F32)


def body(
    tokens, cotangent, routes, route_weights, query_weight, key_weight, value_weight, out_weight,
    gate_weight, up_weight, down_weight, attn_gain, ffn_gain, query_gain, key_gain,
):
    turn = lax.axis_index("tensor").astype(jnp.int32)
    chunk = tokens.shape[0]
    seq = 2 * chunk
    width = tokens.shape[1]
    order = block_order()
    plain = lax.iota(jnp.int32, order.shape[0])
    cosine, sine = rope_tables(seq)
    experts, hidden_cols = gate_weight.shape[2], gate_weight.shape[3]
    flat = experts * hidden_cols
    q_cols, kv_cols = query_weight.shape[2], key_weight.shape[2]
    bits = bits_of(lax.axis_size("dp"))
    straight = list(range(1, bits))
    crossed = straight if bits < 3 else [2, 1] + straight[2:]
    wide, tall = min(512, 2 * kv_cols), min(512, width)

    def select(zero, one):
        return jnp.where(turn == 0, zero, one)

    attn_w = lax.all_gather(
        jnp.concatenate([out_weight[0], query_weight[0], key_weight[0], value_weight[0]], axis=1),
        "dp", axis=0, tiled=True,
    )
    ffn_w = lax.all_gather(
        jnp.concatenate([w[0].reshape(-1, flat) for w in (gate_weight, up_weight, down_weight)], axis=1),
        "dp", axis=0, tiled=True,
    )

    tokens_other = swap_pair(tokens)
    cot_other = swap_pair(after(cotangent, tokens_other))
    (tokens_all,) = join(tokens, tokens_other, turn, plain, 1)
    resid = tokens_all.astype(F32)
    normed = (resid * mean_square(resid) * attn_gain).astype(BF)
    normed_rel = join(normed[:chunk], normed[chunk:], 0, order, 2)

    raw = product(
        dot,
        [(after(normed, normed_rel), (seq, width), lambda i, t: (0, 0))],
        [(attn_w, (width, wide), lambda i, t: (0, q_cols // wide + i))],
        seq, (q_cols + 2 * kv_cols) // wide, wide, F32, turn,
    )
    lse, part, got = {}, {}, {}
    context = None
    for index in (1, 0):
        context, lse[index] = attention_fwd(
            raw, q_cols, kv_cols, chunk, index, query_gain, key_gain, cosine, sine, context
        )
        part[index] = product(
            dot_nt,
            [(in_hbm(context), (chunk, q_cols), lambda i, t, index=index: (index, 0))],
            [(attn_w, (tall, q_cols), lambda i, t: (i, 0))],
            chunk, width // tall, tall, BF, turn,
        )
        got[index] = swap_pair(part[index])
        last = part[index]
        context = after(context, last)

    cot_other = after(cot_other, last)
    (cot_all,) = join(cotangent, cot_other, turn, plain, 1)
    last = cot_all

    mid, back_part, back_got = {}, {}, {}
    normed_f = None
    acts = None
    for index in (1, 0):
        mid[index], normed_f = middle(tokens_all, after(part[index], last), got[index], ffn_gain, index, normed_f)
        acts = expert_part(normed_f, cot_all, ffn_w, routes[0], route_weights[0], index, experts, acts)
        if index == 0:
            ffn_parts_grad = expert_weights(normed_f, cot_all, acts, wide)
            ffn_grad = lax.psum_scatter(ffn_parts_grad, "dp", scatter_dimension=0, tiled=True).astype(F32)
            acts = after(acts, ffn_parts_grad)
        back_part[index] = product(
            dot_nt,
            [(acts, (chunk, 2 * flat), lambda i, t, index=index: (index, 0))],
            [(ffn_w, (tall, 2 * flat), lambda i, t: (i, 0))],
            chunk, width // tall, tall, BF, turn,
        )
        if index == 0:
            back_part[0] = tie(back_part[0], back_got[1])
        back_got[index] = swap_pair(back_part[index])
        last = back_part[index]
        acts, normed_f = after(acts, last), after(normed_f, last)

    def expert_out(who, *needed):
        return product(
            dot_nt,
            [(after(acts, *needed), (chunk, flat), lambda i, t: (who(t[0]), 2))],
            [(ffn_w, (tall, flat), lambda i, t: (i, 2))],
            chunk, width // tall, tall, BF, turn,
        )

    grad_mid, grad_mid_b, ffn_parts, grad_context = {}, {}, {}, {}
    earlier = None
    for index in (1, 0):
        grad_mid[index], grad_mid_b[index], ffn_parts[index] = middle_back(
            cot_all, after(back_part[index], last), back_got[index], mid[index], ffn_gain, index
        )
        grad_context[index] = product(
            dot,
            [(grad_mid_b[index], (chunk, width), lambda i, t: (0, 0))],
            [(attn_w, (width, wide), lambda i, t: (0, i))],
            chunk, q_cols // wide, wide, BF, turn,
        )
        last = grad_context[index]
        if index == 0:
            grad_mid_rel = join(after(grad_mid_b[0], last), grad_mid_b[1], 0, order, 2)
            out_sum = Reduction(grad_mid_rel, context, straight, [])
            out_theirs = expert_out(lambda t: 1 - t, out_sum.sent)
            out_got = swap_pair(tie(out_theirs, back_got[0]))
            last = out_sum.keep(out_theirs)
        dq, dk, dv, query_part, key_part = attention_bwd(
            raw, q_cols, kv_cols, chunk, index, context, after(grad_context[index], last), lse[index],
            query_gain, key_gain, cosine, sine, earlier, index == 0,
        )
        earlier = (dk, dv, query_part, dq)
        last = dq

    dkv = jnp.concatenate([dk, dv], axis=1)

    def normed_back(who, *needed):
        return product(
            dot_nt,
            [
                (after(dq, *needed), (chunk, q_cols), lambda i, t: (who(t[0]), 0)),
                (dkv, (chunk, 2 * kv_cols), lambda i, t: (who(t[0]), 0)),
            ],
            [
                (attn_w, (tall, q_cols), lambda i, t: (i, 1)),
                (attn_w, (tall, 2 * kv_cols), lambda i, t: (i, q_cols // kv_cols)),
            ],
            chunk, width // tall, tall, BF, turn,
        )

    grad_qkv = jnp.concatenate([dq, dkv], axis=1)
    qkv_sum = Reduction(normed_rel, grad_qkv, straight, [])
    grad_theirs = normed_back(lambda t: 1 - t, qkv_sum.sent)
    rest_sum, last = qkv_sum.keep_two(crossed, grad_qkv.shape[1] // 2, grad_theirs)
    grad_got = swap_pair(grad_theirs)
    grad_mine = normed_back(lambda t: t, last)
    out_mine = expert_out(lambda t: t, grad_mine)
    last = out_sum.step(out_mine)
    last = qkv_sum.step(last)
    last = rest_sum.step(last)
    last = out_sum.step(last)
    output = (select(mid[0], mid[1]) + (after(out_mine, last).astype(F32) + out_got.astype(F32))).astype(BF)
    last = qkv_sum.step(output)
    last = rest_sum.step(last)
    grad_normed = after(grad_mine, last).astype(F32) + grad_got.astype(F32)
    tokens_grad = select(grad_mid[0], grad_mid[1]) + norm_back(tokens.astype(F32), attn_gain, grad_normed)[0]

    def gain_part(own, grad):
        values = lax.dynamic_slice_in_dim(tokens_all, own * chunk, chunk, axis=0).astype(F32)
        return jnp.sum(grad.astype(F32) * values * mean_square(values), axis=0, keepdims=True)

    attn_part = gain_part(turn, after(grad_mine, last)) + gain_part(1 - turn, after(grad_theirs, last))
    ffn_part = (ffn_parts[0] + ffn_parts[1]) * 0.5
    small = jnp.concatenate([attn_part, ffn_part, query_part, key_part], axis=1)
    small = tie(small, out_sum.got, rest_sum.got, qkv_sum.got)
    small = sum_all(small)
    out_grad = out_sum.finish(tokens_grad)
    rest_grad = rest_sum.finish(out_grad)
    qkv_grad = jnp.concatenate([qkv_sum.finish(rest_grad), rest_grad], axis=1)

    def expert(index):
        return ffn_grad[:, index * flat : (index + 1) * flat].reshape(1, -1, experts, hidden_cols)

    return (
        output,
        tokens_grad,
        qkv_grad[None, :, :q_cols],
        qkv_grad[None, :, q_cols : q_cols + kv_cols],
        qkv_grad[None, :, q_cols + kv_cols :],
        out_grad[None],
        expert(0),
        expert(1),
        expert(2),
        small[:, :width],
        small[:, width : 2 * width],
        small[:, 2 * width : 2 * width + HD],
        small[:, 2 * width + HD :],
    )


def solution(mesh):
    return jax.shard_map(
        body,
        mesh=mesh,
        in_specs=(
            P(("dp", "tensor"), None),
            P(("dp", "tensor"), None),
            P(None, "dp", None),
            P(None, "dp", None),
            P(None, "dp", "tensor"),
            P(None, "dp", "tensor"),
            P(None, "dp", "tensor"),
            P(None, "dp", "tensor"),
            P(None, "dp", None, "tensor"),
            P(None, "dp", None, "tensor"),
            P(None, "dp", None, "tensor"),
            P(),
            P(),
            P(),
            P(),
        ),
        out_specs=(
            P(("dp", "tensor"), None),
            P(("dp", "tensor"), None),
            P(None, "dp", "tensor"),
            P(None, "dp", "tensor"),
            P(None, "dp", "tensor"),
            P(None, "dp", "tensor"),
            P(None, "dp", None, "tensor"),
            P(None, "dp", None, "tensor"),
            P(None, "dp", None, "tensor"),
            P(),
            P(),
            P(),
            P(),
        ),
        check_vma=False,
    )
```

```python
import functools
import math

import jax
import jax.numpy as jnp
import numpy as np
from jax import lax
from jax.experimental import pallas as pl
from jax.experimental.pallas import tpu as pltpu
from jax.sharding import PartitionSpec as P

HD = 128
EPS = 1e-06
THETA = 1000000.0
SCALE = HD ** -0.5
LOG2E = math.log2(math.e)
NT = (((1,), (1,)), ((), ()))
BF = jnp.bfloat16
F32 = jnp.float32


def params(mib):
    return pltpu.CompilerParams(vmem_limit_bytes=mib * 2**20)


def dot(left, right):
    return jnp.dot(left, right, preferred_element_type=F32)


def dot_nt(left, right):
    return lax.dot_general(left, right, NT, preferred_element_type=F32)


def dot_tn(left, right):
    return lax.dot_general(left, right, (((0,), (0,)), ((), ())), preferred_element_type=F32)


def head_norm(values, gain, cosine, sine):
    scale = lax.rsqrt(jnp.mean(values * values, axis=-1, keepdims=True) + EPS)
    normed = values * scale * gain
    return normed * cosine + pltpu.roll(normed, HD // 2, 1) * sine


def head_norm_back(values, gain, cosine, sine, grad_rot):
    scale = lax.rsqrt(jnp.mean(values * values, axis=-1, keepdims=True) + EPS)
    grad = grad_rot * cosine - pltpu.roll(grad_rot, HD // 2, 1) * sine
    scaled = grad * gain
    inner = jnp.mean(scaled * values, axis=-1, keepdims=True)
    grad_values = scale * scaled - values * (scale * scale * scale) * inner
    return grad_values, jnp.sum(grad * values * scale, axis=0, keepdims=True)


def causal(offset, rows, columns):
    key = lax.broadcasted_iota(jnp.int32, (rows, columns), 0) + offset
    return key <= lax.broadcasted_iota(jnp.int32, (rows, columns), 1)


def attn_fwd_kernel(block, q_ref, k_ref, v_ref, qg_ref, kg_ref, qcos_ref, qsin_ref, kcos_ref, ksin_ref, *rest):
    out_ref, lse_ref, qs, ks, vt, ps, ss, mix, sums = rest[-9:]
    chunk, per = q_ref.shape[0], q_ref.shape[1] // HD
    base = k_ref.shape[0] - chunk
    tile = min(64, block)

    @pl.when(pl.program_id(1) == 0)
    def _():
        ks[...] = head_norm(k_ref[...], kg_ref[...], kcos_ref[...], ksin_ref[...]).astype(BF)
        vt[...] = v_ref[...].astype(BF).T

    for h in range(per):
        lanes = slice(h * HD, (h + 1) * HD)
        qs[h] = head_norm(q_ref[:, lanes], qg_ref[...], qcos_ref[...], qsin_ref[...]).astype(BF)
    pairs = [(h, i) for h in range(per) for i in range(chunk // block)]

    def place(h, i):
        start = base + i * block
        return slice(h * HD, (h + 1) * HD), slice(i * block, (i + 1) * block), start, start + block

    for h, i in pairs:
        lanes, cols, start, end = place(h, i)
        ss[h, :end, cols] = dot_nt(ks[:end], qs[h, cols])
    for h, i in pairs:
        lanes, cols, start, end = place(h, i)
        total = jnp.zeros((8, block), F32)
        for r in range(0, end, tile):
            probs = jnp.exp2(ss[h, r : r + tile, cols] * (SCALE * LOG2E))
            if r >= start:
                probs = jnp.where(causal(r - start, tile, block), probs, 0.0)
            total = total + jnp.sum(probs.reshape(tile // 8, 8, block), axis=0)
            ps[h, r : r + tile, cols] = probs.astype(BF)
        sums[h, :, cols] = jnp.sum(total, axis=0, keepdims=True)
    for h, i in pairs:
        lanes, cols, start, end = place(h, i)
        mix[h, :, cols] = dot(vt[:, :end], ps[h, :end, cols])
    for h, i in pairs:
        lanes, cols, start, end = place(h, i)
        out_ref[cols, lanes] = (mix[h, :, cols] * (1.0 / sums[h, :, cols])).T.astype(BF)
    lse_ref[...] = jnp.log2(sums[...])


def attn_specs(raw, q_cols, kv_cols, chunk, index, per):
    heads, kv = q_cols // HD, kv_cols // HD
    steps = heads // kv // per
    keys = (index + 1) * chunk
    head_in = pl.BlockSpec((chunk, per * HD), lambda k, g: (index, k * steps + g))
    head = pl.BlockSpec((chunk, per * HD), lambda k, g: (0, k * steps + g))
    lse = pl.BlockSpec((per, 1, chunk), lambda k, g: (k * steps + g, 0, 0))
    gain = pl.BlockSpec((1, HD), lambda k, g: (0, 0))
    query_table = pl.BlockSpec((chunk, HD), lambda k, g: (index, 0))

    def of_keys(rows):
        return (
            pl.BlockSpec((rows, HD), lambda k, g: (0, heads + k)),
            pl.BlockSpec((rows, HD), lambda k, g: (0, heads + kv + k)),
            pl.BlockSpec((rows, HD), lambda k, g: (0, 0)),
            pl.BlockSpec((rows, HD), lambda k, g: (0, k)),
        )

    return heads, kv, steps, keys, head_in, head, lse, gain, query_table, of_keys


def attention_fwd(raw, q_cols, kv_cols, chunk, index, query_g, key_g, cosine, sine, earlier):
    seq = raw.shape[0]
    more = [] if earlier is None else [earlier]
    per = min(4, q_cols // kv_cols)
    heads, kv, steps, keys, head_in, head, lse, gain, query_table, of_keys = attn_specs(
        raw, q_cols, kv_cols, chunk, index, per
    )
    key_in, value_in, key_table, _ = of_keys(keys)
    return pl.pallas_call(
        functools.partial(attn_fwd_kernel, min(256, chunk)),
        grid=(kv, steps),
        in_specs=[head_in, key_in, value_in, gain, gain, query_table, query_table, key_table, key_table]
        + [pl.BlockSpec(memory_space=pl.ANY)] * len(more),
        out_specs=[head_in, lse],
        out_shape=[
            pltpu.HBM((seq, heads * HD), BF),
            jax.ShapeDtypeStruct((heads, 1, chunk), F32),
        ],
        scratch_shapes=[
            pltpu.VMEM((per, chunk, HD), BF),
            pltpu.VMEM((keys, HD), BF),
            pltpu.VMEM((HD, keys), BF),
            pltpu.VMEM((per, keys, chunk), BF),
            pltpu.VMEM((per, keys, chunk), F32),
            pltpu.VMEM((per, HD, chunk), F32),
            pltpu.VMEM((per, 1, chunk), F32),
        ],
        input_output_aliases={9: 0} if more else {},
        compiler_params=params(48),
    )(raw, raw, raw, query_g, key_g, cosine, sine, cosine, sine, *more)


def attn_bwd_kernel(
    block, keys, first, last, q_ref, k_ref, v_ref, ctx_ref, grad_ref, lse_ref, qg_ref, kg_ref,
    qcos_ref, qsin_ref, kcos_ref, ksin_ref, *rest,
):
    if first:
        dq_ref, dk_ref, dv_ref, dqg_ref, dkg_ref, qs, ks, kt, vs, ps, ds, dks, dvs, ss, gs, deltas, dqs = rest
    else:
        (dk_in, dv_in, dqg_in, dq_in, dq_ref, dk_ref, dv_ref, dqg_ref, dkg_ref,
         qs, ks, kt, vs, ps, ds, dks, dvs, ss, gs, deltas, dqs) = rest
    chunk, per = q_ref.shape[0], q_ref.shape[1] // HD
    base = (keys - chunk) // block
    kv_id, g_id = pl.program_id(0), pl.program_id(1)

    @pl.when(g_id == 0)
    def _():
        rotated = head_norm(k_ref[:keys], kg_ref[...], kcos_ref[:keys], ksin_ref[:keys]).astype(BF)
        ks[...] = rotated
        kt[...] = rotated.T
        vs[...] = v_ref[:keys].astype(BF)
        dks[...] = jnp.zeros_like(dks) if first else dk_in[...]
        dvs[...] = jnp.zeros_like(dvs) if first else dv_in[...]

    @pl.when((g_id == 0) & (kv_id == 0))
    def _():
        dqg_ref[...] = jnp.zeros_like(dqg_ref) if first else dqg_in[...]
        dkg_ref[...] = jnp.zeros_like(dkg_ref)

    tile = min(64, block)
    for h in range(per):
        lanes = slice(h * HD, (h + 1) * HD)
        qs[h] = head_norm(q_ref[:, lanes], qg_ref[...], qcos_ref[...], qsin_ref[...]).astype(BF)
    pairs = [(h, i) for h in range(per) for i in range(chunk // block)]

    def place(h, i):
        start = (base + i) * block
        return slice(h * HD, (h + 1) * HD), slice(i * block, (i + 1) * block), start, start + block

    def first_products(h):
        for i in range(chunk // block):
            lanes, cols, start, end = place(h, i)
            product = grad_ref[cols, lanes].astype(F32) * ctx_ref[cols, lanes].astype(F32)
            deltas[h, :, cols] = jnp.sum(product.T, axis=0, keepdims=True)
            ss[h % 2, :end, cols] = dot_nt(ks[:end], qs[h, cols])
            gs[h % 2, :end, cols] = dot_nt(vs[:end], grad_ref[cols, lanes])

    def weights(h):
        for i in range(chunk // block):
            lanes, cols, start, end = place(h, i)
            delta, lse = deltas[h, :, cols], lse_ref[h, :, cols]
            for r in range(0, end, tile):
                rows = slice(r, r + tile)
                probs = jnp.exp2(ss[h % 2, rows, cols] * (SCALE * LOG2E) - lse)
                if r >= start:
                    probs = jnp.where(causal(r - start, tile, block), probs, 0.0)
                ps[h % 2, rows, cols] = probs.astype(BF)
                ds[h % 2, rows, cols] = (probs * (gs[h % 2, rows, cols] - delta)).astype(BF)

    def second_products(h):
        lanes = slice(h * HD, (h + 1) * HD)
        for j in range(keys // block):
            rows = slice(j * block, (j + 1) * block)
            start = max(0, j - base) * block
            dvs[rows] += dot(ps[h % 2, rows, start:], grad_ref[start:, lanes])
            dks[rows] += dot(ds[h % 2, rows, start:], qs[h, start:])
        for i in range(chunk // block):
            lanes, cols, start, end = place(h, i)
            dqs[h % 2, :, cols] = dot(kt[:, :end], ds[h % 2, :end, cols])

    def last_part(h):
        total = jnp.zeros((1, HD), F32)
        for i in range(chunk // block):
            lanes, cols, start, end = place(h, i)
            grad_raw, part = head_norm_back(
                q_ref[cols, lanes], qg_ref[...], qcos_ref[cols], qsin_ref[cols], dqs[h % 2, :, cols].T * SCALE
            )
            dq_ref[cols, lanes] = grad_raw.astype(BF)
            total = total + part
        return total

    gain_sum = jnp.zeros((1, HD), F32)
    first_products(0)
    for h in range(per):
        if h + 1 < per:
            first_products(h + 1)
        weights(h)
        if h:
            gain_sum = gain_sum + last_part(h - 1)
        second_products(h)
    gain_sum = gain_sum + last_part(per - 1)
    dqg_ref[...] += gain_sum

    @pl.when(g_id == pl.num_programs(1) - 1)
    def _():
        if last:
            grad_raw, part = head_norm_back(k_ref[...], kg_ref[...], kcos_ref[...], ksin_ref[...], dks[...] * SCALE)
            dk_ref[...] = grad_raw.astype(BF)
            dv_ref[...] = dvs[...].astype(BF)
            dkg_ref[...] += part
        else:
            dk_ref[...] = dks[...]
            dv_ref[...] = dvs[...]


def attention_bwd(
    raw, q_cols, kv_cols, chunk, index, context, grad_context, lse_rows, query_g, key_g, cosine, sine, earlier, last
):
    seq = raw.shape[0]
    per = min(4, q_cols // kv_cols)
    heads, kv, steps, keys, head_in, head, lse, gain, query_table, of_keys = attn_specs(
        raw, q_cols, kv_cols, chunk, index, per
    )
    key_in, value_in, key_table, key_out = of_keys(seq)
    first = earlier is None
    more = [] if first else list(earlier)
    kind = BF if last else F32
    return pl.pallas_call(
        functools.partial(attn_bwd_kernel, min(256, chunk), keys, first, last),
        grid=(kv, steps),
        in_specs=[head_in, key_in, value_in, head_in, head, lse, gain, gain, query_table, query_table, key_table, key_table]
        + ([] if first else [key_out, key_out, gain, pl.BlockSpec(memory_space=pl.ANY)]),
        out_specs=[head_in, key_out, key_out, gain, gain],
        out_shape=[
            jax.ShapeDtypeStruct((seq, heads * HD), BF),
            jax.ShapeDtypeStruct((seq, kv * HD), kind),
            jax.ShapeDtypeStruct((seq, kv * HD), kind),
            jax.ShapeDtypeStruct((1, HD), F32),
            jax.ShapeDtypeStruct((1, HD), F32),
        ],
        scratch_shapes=[
            pltpu.VMEM((per, chunk, HD), BF),
            pltpu.VMEM((keys, HD), BF),
            pltpu.VMEM((HD, keys), BF),
            pltpu.VMEM((keys, HD), BF),
            pltpu.VMEM((2, keys, chunk), BF),
            pltpu.VMEM((2, keys, chunk), BF),
            pltpu.VMEM((seq, HD), F32),
            pltpu.VMEM((seq, HD), F32),
            pltpu.VMEM((2, keys, chunk), F32),
            pltpu.VMEM((2, keys, chunk), F32),
            pltpu.VMEM((per, 1, chunk), F32),
            pltpu.VMEM((2, HD, chunk), F32),
        ],
        input_output_aliases={} if first else {15: 0},
        compiler_params=params(58),
    )(raw, raw, raw, in_hbm(context), grad_context, lse_rows, query_g, key_g, cosine, sine, cosine, sine, *more)


def rope_tables(seq):
    position = lax.iota(F32, seq)
    freq = THETA ** (-2.0 * lax.iota(F32, HD // 2) / HD)
    angle = position[:, None] * freq[None, :]
    cosine, sine = jnp.cos(angle), jnp.sin(angle)
    return jnp.concatenate([cosine, cosine], axis=1), jnp.concatenate([-sine, sine], axis=1)


def bits_of(count):
    return count.bit_length() - 1


def swap(value, bit):
    count = lax.axis_size("dp")
    return lax.ppermute(value, "dp", [(i, i ^ (1 << bit)) for i in range(count)])


def swap_pair(value):
    return lax.ppermute(value, "tensor", [(0, 1), (1, 0)])


def after(value, *needed):
    return lax.optimization_barrier((value, needed))[0]


def in_hbm(value):
    return pltpu.with_memory_space_constraint(value, pltpu.HBM)


def tie_kernel(*refs):
    pass


def tie(value, *needed):
    anywhere = pl.BlockSpec(memory_space=pl.ANY)
    return pl.pallas_call(
        tie_kernel,
        in_specs=[anywhere] * (1 + len(needed)),
        out_specs=anywhere,
        out_shape=jax.ShapeDtypeStruct(value.shape, value.dtype),
        input_output_aliases={0: 0},
    )(value, *needed)


def block_order():
    count = lax.axis_size("dp")
    bits = bits_of(count)
    reverse = np.array([int(format(i, "b").zfill(bits)[::-1], 2) if bits else 0 for i in range(count)], np.int32)
    return jnp.asarray(reverse) ^ lax.axis_index("dp").astype(jnp.int32)


def join_kernel(count, parts, turn_ref, order_ref, one_ref, two_ref, *out_refs):
    block = one_ref.shape[1] // count

    def fill(ref):
        for i in range(count):
            column = pl.multiple_of(order_ref[i] * block, block)
            out_ref, at = out_refs[i // (count // parts)], i % (count // parts)
            out_ref[:, at * block : (at + 1) * block] = ref[:, pl.ds(column, block)]

    @pl.when(pl.program_id(0) == turn_ref[0])
    def _():
        fill(one_ref)

    @pl.when(pl.program_id(0) != turn_ref[0])
    def _():
        fill(two_ref)


def join(one, two, turn, order, parts):
    rows, width = one.shape
    count = order.shape[0]
    tile = min(256, rows)
    turn = jnp.asarray(turn, jnp.int32)
    if (width // count) % 128:
        both = jnp.where(turn == 0, jnp.concatenate([one, two], axis=0), jnp.concatenate([two, one], axis=0))
        both = jnp.take(both.reshape(2 * rows, count, -1), order, axis=1).reshape(2 * rows, width)
        return jnp.split(both, parts, axis=1)
    steps = rows // tile
    half = pl.BlockSpec((tile, width), lambda h, r: (r, 0))
    scalar = pl.BlockSpec(memory_space=pltpu.SMEM)
    return pl.pallas_call(
        functools.partial(join_kernel, count, parts),
        grid=(2, steps),
        in_specs=[scalar, scalar, half, half],
        out_specs=[pl.BlockSpec((tile, width // parts), lambda h, r: (h * steps + r, 0))] * parts,
        out_shape=[jax.ShapeDtypeStruct((2 * rows, width // parts), one.dtype)] * parts,
        compiler_params=params(32),
    )(turn.reshape(1), order, one, two)


def mean_square(values):
    return lax.rsqrt(jnp.mean(values * values, axis=-1, keepdims=True) + EPS)


def mid_kernel(base_ref, part_ref, got_ref, gain_ref, *rest):
    mid_ref, normed_ref = rest[-2:]
    mid = base_ref[...].astype(F32) + (part_ref[...].astype(F32) + got_ref[...].astype(F32))
    mid_ref[...] = mid
    normed_ref[...] = (mid * mean_square(mid) * gain_ref[...]).astype(BF)


def middle(base, part, got, gain, index, earlier):
    rows, width = part.shape
    tile = min(128, rows)
    block = pl.BlockSpec((tile, width), lambda r: (r, 0))
    place = pl.BlockSpec((tile, width), lambda r: (index * (rows // tile) + r, 0))
    more = [] if earlier is None else [earlier]
    return pl.pallas_call(
        mid_kernel,
        grid=(rows // tile,),
        in_specs=[place, block, block, pl.BlockSpec((1, width), lambda r: (0, 0))]
        + [pl.BlockSpec(memory_space=pl.ANY)] * len(more),
        out_specs=[block, place],
        out_shape=[pltpu.HBM((rows, width), F32), pltpu.HBM(base.shape, BF)],
        input_output_aliases={4: 1} if more else {},
        compiler_params=params(32),
    )(base, part, got, gain, *more)


def norm_back(values, gain, grad):
    scale = mean_square(values)
    scaled = grad * gain
    inner = jnp.mean(scaled * values, axis=-1, keepdims=True)
    grad_values = scale * scaled - values * (scale * scale * scale) * inner
    return grad_values, jnp.sum(grad * values * scale, axis=0, keepdims=True)


def mid_back_kernel(base_ref, part_ref, got_ref, mid_ref, gain_ref, out_ref, low_ref, sum_ref):
    grad = part_ref[...].astype(F32) + got_ref[...].astype(F32)
    back, part = norm_back(mid_ref[...], gain_ref[...], grad)
    total = base_ref[...].astype(F32) + back
    out_ref[...] = total
    low_ref[...] = total.astype(BF)

    @pl.when(pl.program_id(0) == 0)
    def _():
        sum_ref[...] = jnp.zeros_like(sum_ref)

    sum_ref[...] += part


def middle_back(base, part, got, mid, gain, index):
    rows, width = part.shape
    tile = min(128, rows)
    block = pl.BlockSpec((tile, width), lambda r: (r, 0))
    line = pl.BlockSpec((1, width), lambda r: (0, 0))
    return pl.pallas_call(
        mid_back_kernel,
        grid=(rows // tile,),
        in_specs=[pl.BlockSpec((tile, width), lambda r: (index * (rows // tile) + r, 0)), block, block, block, line],
        out_specs=[block, block, line],
        out_shape=[
            pltpu.HBM((rows, width), F32),
            jax.ShapeDtypeStruct((rows, width), BF),
            jax.ShapeDtypeStruct((1, width), F32),
        ],
        compiler_params=params(32),
    )(base, part, got, in_hbm(mid), gain)


def expert_kernel(unit, cols, x_ref, cot_ref, gate_ref, up_ref, down_ref, route_ref, weight_ref, *rest):
    out_ref = rest[-1]
    step, count = pl.program_id(0), pl.num_programs(0)
    rows, block = x_ref.shape[0], gate_ref.shape[1]
    tile = min(256, rows)

    def place(kind):
        return pl.ds(pl.multiple_of((kind * count + step) * block, block), block)

    for r in range(rows // tile):
        part = slice(r * tile, (r + 1) * tile)
        shares = []
        for k in range(block // unit):
            expert = (step * (block // unit) + k) // (cols // unit)
            share = jnp.sum(jnp.where(route_ref[part] == expert, weight_ref[part], 0.0), axis=-1, keepdims=True)
            shares.append(jnp.broadcast_to(share, (tile, unit)))
        share = jnp.concatenate(shares, axis=1)
        gate = dot(x_ref[part], gate_ref[...])
        up = dot(x_ref[part], up_ref[...])
        grad_hidden = dot(cot_ref[part], down_ref[...]) * share
        sigma = 1.0 / (1.0 + jnp.exp(-gate))
        silu = gate * sigma
        out_ref[part, place(0)] = (grad_hidden * up * (sigma + silu * (1.0 - sigma))).astype(BF)
        out_ref[part, place(1)] = (grad_hidden * silu).astype(BF)
        out_ref[part, place(2)] = (silu * up * share).astype(BF)


def expert_part(normed, cot, weights, routes, route_weights, index, experts, earlier):
    width = normed.shape[1]
    flat = weights.shape[1] // 3
    cols = flat // experts
    unit = math.gcd(cols, 128)
    block = 2 * unit if flat % (2 * unit) == 0 else unit
    steps = flat // block
    seq = routes.shape[0]
    rows = seq // 2
    pair = pl.BlockSpec((rows, routes.shape[1]), lambda e: (index, 0))
    half = pl.BlockSpec((rows, width), lambda e: (index, 0))
    more = [] if earlier is None else [earlier]
    return pl.pallas_call(
        functools.partial(expert_kernel, unit, cols),
        grid=(steps,),
        in_specs=[half, half]
        + [pl.BlockSpec((width, block), lambda e, k=k: (0, k * steps + e)) for k in range(3)]
        + [pair, pair]
        + [pl.BlockSpec(memory_space=pl.ANY)] * len(more),
        out_specs=pl.BlockSpec((rows, 3 * flat), lambda e: (index, 0)),
        out_shape=jax.ShapeDtypeStruct((seq, 3 * flat), BF),
        input_output_aliases={7: 0} if more else {},
        compiler_params=params(56),
    )(in_hbm(normed), cot, weights, weights, weights, routes, route_weights, *more)


def expert_weight_kernel(cut, normed_ref, cot_ref, act_ref, out_ref):
    step = pl.program_id(0)

    @pl.when(step < cut)
    def _():
        out_ref[...] = dot_tn(normed_ref[...], act_ref[...]).astype(BF)

    @pl.when(step >= cut)
    def _():
        out_ref[...] = dot_tn(cot_ref[...], act_ref[...]).astype(BF)


def expert_weights(normed, cot, acts, block):
    seq, width = normed.shape
    flat = acts.shape[1] // 3
    full = pl.BlockSpec((seq, width), lambda j: (0, 0))
    return pl.pallas_call(
        functools.partial(expert_weight_kernel, 2 * flat // block),
        grid=(3 * flat // block,),
        in_specs=[full, full, pl.BlockSpec((seq, block), lambda j: (0, j))],
        out_specs=pl.BlockSpec((width, block), lambda j: (0, j)),
        out_shape=jax.ShapeDtypeStruct((width, 3 * flat), BF),
        compiler_params=params(56),
    )(in_hbm(normed), cot, acts)


def product_kernel(count, form, turn_ref, *refs):
    total = form(refs[0][...], refs[count][...])
    for i in range(1, count):
        total = total + form(refs[i][...], refs[count + i][...])
    refs[-1][...] = total.astype(refs[-1].dtype)


def product(form, lefts, rights, rows, steps, block, kind, turn, needed=()):
    return pl.pallas_call(
        functools.partial(product_kernel, len(lefts), form),
        grid_spec=pltpu.PrefetchScalarGridSpec(
            num_scalar_prefetch=1,
            grid=(steps,),
            in_specs=[pl.BlockSpec(shape, index) for _, shape, index in lefts + rights]
            + [pl.BlockSpec(memory_space=pl.ANY)] * len(needed),
            out_specs=pl.BlockSpec((rows, block), lambda i, turn_ref: (0, i)),
        ),
        out_shape=jax.ShapeDtypeStruct((rows, steps * block), kind),
        compiler_params=params(56),
    )(turn.reshape(1), *[item[0] for item in lefts + rights], *needed)


def fold(keep, received):
    return (keep.astype(F32) + received.astype(F32)).astype(BF)


def sum_all(value):
    for bit in range(bits_of(lax.axis_size("dp"))):
        value = value + swap(value, bit)
    return value + swap_pair(value)


class Reduction:
    def __init__(self, lefts, right, order, ready, *needed):
        self.order = list(order)
        self.lefts, self.right = lefts, right
        self.rows = 2 * lefts[0].shape[1] // lax.axis_size("dp")
        self.axes = list(range(1, bits_of(lax.axis_size("dp"))))
        self.sent = dot_tn(after(lefts[1], *needed), right).astype(BF)
        self.got = swap(tie(self.sent, *ready), 0)

    def total(self, *needed):
        total = dot_tn(after(self.lefts[0], *needed), self.right) + self.got.astype(F32)
        return total.astype(BF).reshape((2,) * len(self.axes) + (self.rows, -1))

    def keep(self, *needed):
        held = self.total(*needed)
        self.send(held)
        return held

    def keep_two(self, other, cut, *needed):
        held = self.total(*needed)
        rest = Reduction.__new__(Reduction)
        rest.order, rest.axes = list(other), list(self.axes)
        self.send(held[..., :cut])
        rest.send(held[..., cut:])
        return rest, held

    def send(self, held):
        axis = self.axes.index(self.order[0])
        self.mine = lax.index_in_dim(held, 0, axis, keepdims=False)
        self.got = swap(lax.index_in_dim(held, 1, axis, keepdims=False), self.order[0])

    def fold(self, *needed):
        self.axes.remove(self.order.pop(0))
        mine = after(self.mine, *needed) if needed else self.mine
        return fold(mine, self.got)

    def step(self, *needed):
        held = self.fold(*needed)
        self.send(held)
        return held

    def join(self, other, *needed):
        held = jnp.concatenate([self.fold(*needed), other.fold(*needed)], axis=-1)
        self.send(held)
        return held

    def finish(self, *needed):
        while len(self.order) > 1:
            self.step(*needed)
        self.axes.remove(self.order.pop(0))
        return after(self.mine, *needed).astype(F32) + self.got.astype(F32)


def body(
    tokens, cotangent, routes, route_weights, query_weight, key_weight, value_weight, out_weight,
    gate_weight, up_weight, down_weight, attn_gain, ffn_gain, query_gain, key_gain,
):
    turn = lax.axis_index("tensor").astype(jnp.int32)
    chunk = tokens.shape[0]
    seq = 2 * chunk
    width = tokens.shape[1]
    order = block_order()
    plain = lax.iota(jnp.int32, order.shape[0])
    cosine, sine = rope_tables(seq)
    experts, hidden_cols = gate_weight.shape[2], gate_weight.shape[3]
    flat = experts * hidden_cols
    q_cols, kv_cols = query_weight.shape[2], key_weight.shape[2]
    bits = bits_of(lax.axis_size("dp"))
    straight = list(range(1, bits))
    crossed = straight if bits < 3 else [2, 1] + straight[2:]
    wide, tall = min(512, 2 * kv_cols), min(512, width)

    def select(zero, one):
        return jnp.where(turn == 0, zero, one)

    attn_w = lax.all_gather(
        jnp.concatenate([out_weight[0], query_weight[0], key_weight[0], value_weight[0]], axis=1),
        "dp", axis=0, tiled=True,
    )
    ffn_w = lax.all_gather(
        jnp.concatenate([w[0].reshape(-1, flat) for w in (gate_weight, up_weight, down_weight)], axis=1),
        "dp", axis=0, tiled=True,
    )

    tokens_other = swap_pair(tokens)
    cot_other = swap_pair(after(cotangent, tokens_other))
    (tokens_all,) = join(tokens, tokens_other, turn, plain, 1)
    resid = tokens_all.astype(F32)
    normed = (resid * mean_square(resid) * attn_gain).astype(BF)
    normed_rel = join(normed[:chunk], normed[chunk:], 0, order, 2)

    raw = product(
        dot,
        [(after(normed, normed_rel), (seq, width), lambda i, t: (0, 0))],
        [(attn_w, (width, wide), lambda i, t: (0, q_cols // wide + i))],
        seq, (q_cols + 2 * kv_cols) // wide, wide, F32, turn,
    )
    lse, part, got = {}, {}, {}
    context = None
    for index in (1, 0):
        context, lse[index] = attention_fwd(
            raw, q_cols, kv_cols, chunk, index, query_gain, key_gain, cosine, sine, context
        )
        part[index] = product(
            dot_nt,
            [(in_hbm(context), (chunk, q_cols), lambda i, t, index=index: (index, 0))],
            [(attn_w, (tall, q_cols), lambda i, t: (i, 0))],
            chunk, width // tall, tall, BF, turn,
        )
        got[index] = swap_pair(part[index])
        last = part[index]
        context = after(context, last)

    cot_other = after(cot_other, last)
    (cot_all,) = join(cotangent, cot_other, turn, plain, 1)
    last = cot_all

    mid, back_part, back_got = {}, {}, {}
    normed_f = None
    acts = None
    for index in (1, 0):
        mid[index], normed_f = middle(tokens_all, after(part[index], last), got[index], ffn_gain, index, normed_f)
        acts = expert_part(normed_f, cot_all, ffn_w, routes[0], route_weights[0], index, experts, acts)
        if index == 0:
            ffn_parts_grad = expert_weights(normed_f, cot_all, acts, wide)
            ffn_grad = lax.psum_scatter(ffn_parts_grad, "dp", scatter_dimension=0, tiled=True).astype(F32)
            acts = after(acts, ffn_parts_grad)
        back_part[index] = product(
            dot_nt,
            [(acts, (chunk, 2 * flat), lambda i, t, index=index: (index, 0))],
            [(ffn_w, (tall, 2 * flat), lambda i, t: (i, 0))],
            chunk, width // tall, tall, BF, turn,
        )
        if index == 0:
            back_part[0] = tie(back_part[0], back_got[1])
        back_got[index] = swap_pair(back_part[index])
        last = back_part[index]
        acts, normed_f = after(acts, last), after(normed_f, last)

    def expert_out(who, *needed):
        return product(
            dot_nt,
            [(acts, (chunk, flat), lambda i, t: (who(t[0]), 2))],
            [(ffn_w, (tall, flat), lambda i, t: (i, 2))],
            chunk, width // tall, tall, BF, turn, needed,
        )

    grad_mid, grad_mid_b, ffn_parts, grad_context = {}, {}, {}, {}
    earlier = None
    for index in (1, 0):
        grad_mid[index], grad_mid_b[index], ffn_parts[index] = middle_back(
            cot_all, after(back_part[index], last), back_got[index], mid[index], ffn_gain, index
        )
        grad_context[index] = product(
            dot,
            [(grad_mid_b[index], (chunk, width), lambda i, t: (0, 0))],
            [(attn_w, (width, wide), lambda i, t: (0, i))],
            chunk, q_cols // wide, wide, BF, turn,
        )
        last = grad_context[index]
        if index == 0:
            grad_mid_rel = join(after(grad_mid_b[0], last), grad_mid_b[1], 0, order, 2)
            out_sum = Reduction(grad_mid_rel, context, straight, [])
            last = out_sum.keep(out_sum.sent)
        dq, dk, dv, query_part, key_part = attention_bwd(
            raw, q_cols, kv_cols, chunk, index, context, after(grad_context[index], last), lse[index],
            query_gain, key_gain, cosine, sine, earlier, index == 0,
        )
        earlier = (dk, dv, query_part, dq)
        last = dq

    dkv = jnp.concatenate([dk, dv], axis=1)

    def normed_back(who, *needed):
        return product(
            dot_nt,
            [
                (after(dq, *needed), (chunk, q_cols), lambda i, t: (who(t[0]), 0)),
                (dkv, (chunk, 2 * kv_cols), lambda i, t: (who(t[0]), 0)),
            ],
            [
                (attn_w, (tall, q_cols), lambda i, t: (i, 1)),
                (attn_w, (tall, 2 * kv_cols), lambda i, t: (i, q_cols // kv_cols)),
            ],
            chunk, width // tall, tall, BF, turn,
        )

    grad_qkv = jnp.concatenate([dq, dkv], axis=1)
    qkv_sum = Reduction(normed_rel, grad_qkv, straight, [])
    grad_theirs = normed_back(lambda t: 1 - t, qkv_sum.sent)
    rest_sum, last = qkv_sum.keep_two(crossed, grad_qkv.shape[1] // 2, grad_theirs)
    grad_got = swap_pair(grad_theirs)
    grad_mine = normed_back(lambda t: t, last)
    out_theirs = expert_out(lambda t: 1 - t, grad_mine)
    out_got = swap_pair(out_theirs)
    out_mine = expert_out(lambda t: t, out_theirs)
    last = out_sum.step(out_mine)
    last = qkv_sum.step(last)
    last = rest_sum.step(last)
    last = out_sum.step(last)
    output = (select(mid[0], mid[1]) + (after(out_mine, last).astype(F32) + out_got.astype(F32))).astype(BF)
    last = qkv_sum.step(output)
    last = rest_sum.step(last)
    grad_normed = after(grad_mine, last).astype(F32) + grad_got.astype(F32)
    tokens_grad = select(grad_mid[0], grad_mid[1]) + norm_back(tokens.astype(F32), attn_gain, grad_normed)[0]

    def gain_part(own, grad):
        values = lax.dynamic_slice_in_dim(tokens_all, own * chunk, chunk, axis=0).astype(F32)
        return jnp.sum(grad.astype(F32) * values * mean_square(values), axis=0, keepdims=True)

    attn_part = gain_part(turn, after(grad_mine, last)) + gain_part(1 - turn, after(grad_theirs, last))
    ffn_part = (ffn_parts[0] + ffn_parts[1]) * 0.5
    small = jnp.concatenate([attn_part, ffn_part, query_part, key_part], axis=1)
    small = tie(small, out_sum.got, rest_sum.got, qkv_sum.got)
    small = sum_all(small)
    out_grad = out_sum.finish(tokens_grad)
    rest_grad = rest_sum.finish(out_grad)
    qkv_grad = jnp.concatenate([qkv_sum.finish(rest_grad), rest_grad], axis=1)

    def expert(index):
        return ffn_grad[:, index * flat : (index + 1) * flat].reshape(1, -1, experts, hidden_cols)

    return (
        output,
        tokens_grad,
        qkv_grad[None, :, :q_cols],
        qkv_grad[None, :, q_cols : q_cols + kv_cols],
        qkv_grad[None, :, q_cols + kv_cols :],
        out_grad[None],
        expert(0),
        expert(1),
        expert(2),
        small[:, :width],
        small[:, width : 2 * width],
        small[:, 2 * width : 2 * width + HD],
        small[:, 2 * width + HD :],
    )


def solution(mesh):
    return jax.shard_map(
        body,
        mesh=mesh,
        in_specs=(
            P(("dp", "tensor"), None),
            P(("dp", "tensor"), None),
            P(None, "dp", None),
            P(None, "dp", None),
            P(None, "dp", "tensor"),
            P(None, "dp", "tensor"),
            P(None, "dp", "tensor"),
            P(None, "dp", "tensor"),
            P(None, "dp", None, "tensor"),
            P(None, "dp", None, "tensor"),
            P(None, "dp", None, "tensor"),
            P(),
            P(),
            P(),
            P(),
        ),
        out_specs=(
            P(("dp", "tensor"), None),
            P(("dp", "tensor"), None),
            P(None, "dp", "tensor"),
            P(None, "dp", "tensor"),
            P(None, "dp", "tensor"),
            P(None, "dp", "tensor"),
            P(None, "dp", None, "tensor"),
            P(None, "dp", None, "tensor"),
            P(None, "dp", None, "tensor"),
            P(),
            P(),
            P(),
            P(),
        ),
        check_vma=False,
    )
```
